128 devices in a mesh: rows: 4 (over y_hi, core), loop: 32 (over z, x, y_lo).
Axes of the slice: x: 4, y: 4 (y_hi: 2, y_lo: 2; y = y_hi * 2 + y_lo), z: 4, core: 2. Of those that a mesh axis runs over, the one named last changes fastest.
Arguments:
- delta_weight_matrix: float32 [98304, 4096], P('rows', 'loop'), may hold values from -18 to 18
- offsets: int32 [2, 4], replicated, may hold values from 0 to 63, as said below
Outputs:
- rotated: float32 [98304, 4096], P('rows', 'loop')
The draws below stay inside these ranges and needn't reach their ends.
Inputs may be any that keep to these rules, and one draw needn't show every extreme that they name: The 4 offsets of each step are distinct.
All inputs are finite; a program needn't handle non-finite values.
Results may differ from the reference program's by a relative error of at most 0.0003.
Values sent between devices are 32-bit elements; how exact they have to be, the bound alone decides.
No kernel may reach another device: no remote copies, remote signals or barrier semaphores. Data moves between devices by JAX's collectives and lax.ppermute only.
A program may use at most 128 MiB of HBM per device.

```python
import math
import jax
import jax.numpy as jnp
from jax import lax

BLOCK_COLS = 64
INNER_ROUNDS = 4
SWEEP_STEPS = 2
TOTAL_ROWS = 98304
COLUMNS = 4096
N_LOOP = 32


def draw_delta_weight_matrix(key, part):
    key = jax.random.fold_in(key, 11)
    key_entries, key_cols = jax.random.split(key, 2)
    scales = jnp.exp(jax.random.uniform(key_cols, (COLUMNS,), jnp.float32, math.log(0.3), math.log(3.0)))
    entries = jnp.clip(jax.random.normal(key_entries, (TOTAL_ROWS, COLUMNS), jnp.float32), -6.0, 6.0)
    values = entries * scales
    return values.astype(jnp.float32)


def draw_offsets(key, part):
    key = jax.random.fold_in(key, 23)
    step_keys = jax.random.split(key, 2 * SWEEP_STEPS)
    rows_list = []
    for which in range(SWEEP_STEPS):
        order = jax.random.permutation(step_keys[2 * which], BLOCK_COLS - 1).astype(jnp.int32)
        picked = jnp.concatenate([order[:INNER_ROUNDS - 1], jnp.full((1,), BLOCK_COLS - 1, jnp.int32)], 0)
        placed = jax.random.permutation(step_keys[2 * which + 1], picked)
        rows_list.append(placed.astype(jnp.int32))
    return jnp.stack(rows_list, 0).astype(jnp.int32)


def setup_inputs(seed: int = 0) -> dict:
    key_list = jax.random.split(jax.random.key(seed), 3)
    return {
        "delta_weight_matrix": draw_delta_weight_matrix(jax.random.fold_in(key_list[2], 71), 0),
        "offsets": draw_offsets(jax.random.fold_in(key_list[2], 71), 0),
    }


PRECISION_HIGH = lax.Precision.HIGHEST

def paired_gram_matrix(left, right):
    return lax.dot_general(left, right, (((0,), (0,)), ((), ())), precision=PRECISION_HIGH, preferred_element_type=jnp.float32)

def jacobi_rotations(gram_matrix, circle_shifts):
    block_width = gram_matrix.shape[0]
    half = block_width // 2
    right_vectors = jnp.eye(block_width, dtype=gram_matrix.dtype)
    column = jnp.arange(half, dtype=jnp.int32)
    for which in range(INNER_ROUNDS):
        partner = half + (column + circle_shifts[which].astype(jnp.int32)) % half
        g_first = gram_matrix[column, column]
        g_second = gram_matrix[partner, partner]
        g_cross = gram_matrix[column, partner]
        spread = g_second - g_first
        sign_part = jnp.where(spread >= 0.0, 1.0, -1.0).astype(gram_matrix.dtype)
        tangent = sign_part * 2.0 * g_cross / (jnp.abs(spread) + jnp.sqrt(spread * spread + 4.0 * g_cross * g_cross))
        cosine = 1.0 / jnp.sqrt(1.0 + tangent * tangent)
        sine = -tangent * cosine
        rotate_pair = jnp.zeros((block_width, block_width), gram_matrix.dtype)
        rotate_pair = rotate_pair.at[column, column].set(cosine).at[partner, partner].set(cosine)
        rotate_pair = rotate_pair.at[partner, column].set(sine).at[column, partner].set(-sine)
        gram_matrix = jnp.dot(rotate_pair.T, jnp.dot(gram_matrix, rotate_pair, precision=PRECISION_HIGH), precision=PRECISION_HIGH)
        right_vectors = jnp.dot(right_vectors, rotate_pair, precision=PRECISION_HIGH)
    return (right_vectors, gram_matrix)

def reference(delta_weight_matrix, offsets):
    half = BLOCK_COLS
    pairs = delta_weight_matrix.reshape(TOTAL_ROWS, N_LOOP, 2 * half).transpose(1, 0, 2)

    def one_step(stack, circle_shifts):

        def single(column_block):
            right_vectors, discarded_value = jacobi_rotations(paired_gram_matrix(column_block, column_block), circle_shifts)
            return jnp.dot(column_block, right_vectors, precision=PRECISION_HIGH, preferred_element_type=jnp.float32)
        return lax.map(single, stack)
    pairs = one_step(pairs, offsets[0])
    firsts = pairs[:, :, :half]
    seconds = pairs[:, :, half:]
    new_first = jnp.concatenate([firsts[:1], seconds[:1], firsts[1:N_LOOP - 1]], 0)
    new_second = jnp.concatenate([seconds[1:], firsts[N_LOOP - 1:]], 0)
    pairs = jnp.concatenate([new_first, new_second], 2)
    pairs = one_step(pairs, offsets[1])
    return pairs.transpose(1, 0, 2).reshape(TOTAL_ROWS, COLUMNS)
```

```python
import functools

import jax
import jax.numpy as jnp
from jax import lax
from jax.experimental import pallas as pl
from jax.experimental.pallas import tpu as pltpu
from jax.sharding import PartitionSpec as P

ROUNDS = 4
MIB = 1024 * 1024
F32 = jnp.float32
BF16 = jnp.bfloat16


def params(mib=58):
    return pltpu.CompilerParams(vmem_limit_bytes=mib * MIB)


def parts(x):
    high = x.astype(BF16)
    low = (x - high.astype(F32)).astype(BF16)
    return high, low


def gram_terms(x):
    high, low = parts(x)
    return lax.dot_general(
        high,
        jnp.concatenate([high, low], axis=1),
        (((0,), (0,)), ((), ())),
        preferred_element_type=F32,
    )


def gram_of_terms(terms):
    width = terms.shape[0]
    cross = terms[:, width:]
    return terms[:, :width] + cross + cross.T


def swapped(x, axis):
    return pltpu.roll(x, x.shape[axis] // 2, axis)


def times(x, weights):
    width = x.shape[1]
    both = jnp.dot(
        jnp.concatenate(parts(x), axis=1), weights, preferred_element_type=F32
    )
    return both[:, :width] + both[:, width:]


def left_lanes(shape):
    return lax.broadcasted_iota(jnp.int32, shape, 1) < shape[1] // 2


def gram_kernel(x_ref, gram_ref, terms_ref):
    step = pl.program_id(0)

    @pl.when(step == 0)
    def _():
        terms_ref[...] = jnp.zeros_like(terms_ref)

    terms_ref[...] += gram_terms(x_ref[...])

    @pl.when(step == pl.num_programs(0) - 1)
    def _():
        gram_ref[...] = gram_of_terms(terms_ref[...])


def local_gram(x, block):
    rows, width = x.shape
    return pl.pallas_call(
        gram_kernel,
        grid=(rows // block,),
        in_specs=[pl.BlockSpec((block, width), lambda i: (i, 0))],
        out_specs=pl.BlockSpec((width, width), lambda i: (0, 0)),
        out_shape=jax.ShapeDtypeStruct((width, width), F32),
        scratch_shapes=[pltpu.VMEM((width, 2 * width), F32)],
        compiler_params=params(),
    )(x)


def rotation_kernel(which, flags_ref, offsets_ref, one_ref, two_ref, a_ref, b_ref):
    gram = one_ref[...] + two_ref[...]
    width = gram.shape[0]
    half = width // 2
    row = lax.broadcasted_iota(jnp.int32, (width, width), 0)
    lane = lax.broadcasted_iota(jnp.int32, (width, width), 1)
    eye = row == lane
    is_first = lax.broadcasted_iota(jnp.int32, (1, width), 1) < half
    vectors = jnp.where(eye, 1.0, 0.0).astype(F32)
    dot = functools.partial(
        jnp.dot, precision=lax.Precision.HIGHEST, preferred_element_type=F32
    )
    for turn in range(ROUNDS):
        offset = offsets_ref[which, turn]
        above = lane + offset
        above = half + jnp.where(above >= half, above - half, above)
        below = lane - half - offset
        below = jnp.where(below < 0, below + half, below)
        pair = row == jnp.where(lane < half, above, below)
        own = jnp.sum(jnp.where(eye, gram, 0.0), axis=0, keepdims=True)
        own_col = jnp.sum(jnp.where(eye, gram, 0.0), axis=1, keepdims=True)
        other = jnp.sum(jnp.where(pair, own_col, 0.0), axis=0, keepdims=True)
        cross = jnp.sum(jnp.where(pair, gram, 0.0), axis=0, keepdims=True)
        spread = jnp.where(is_first, other - own, own - other)
        sign = jnp.where(spread >= 0.0, 1.0, -1.0)
        tangent = (
            sign
            * 2.0
            * cross
            / (jnp.abs(spread) + jnp.sqrt(spread * spread + 4.0 * cross * cross))
        )
        cosine = 1.0 / jnp.sqrt(1.0 + tangent * tangent)
        sine = tangent * cosine
        signed = jnp.where(is_first, -sine, sine)
        on_diagonal = jnp.where(eye, cosine, 0.0)
        off_diagonal = jnp.where(pair, signed, 0.0)
        turned = on_diagonal + off_diagonal
        vectors = dot(vectors, turned)
        if turn < ROUNDS - 1:
            gram = dot(on_diagonal - off_diagonal, dot(gram, turned))
    if which == 0:
        vectors = jnp.where(flags_ref[0] == 1, swapped(vectors, 1), vectors)
        other_vectors = swapped(vectors, 1)
    else:
        other_vectors = swapped(vectors, 0)
    for out_ref, v in ((a_ref, vectors), (b_ref, other_vectors)):
        both = jnp.concatenate(parts(v), axis=1)
        out_ref[...] = jnp.concatenate([both, both], axis=0)


def rotations(which, flags, offsets, one, two):
    width = one.shape[0]
    smem = pl.BlockSpec(memory_space=pltpu.SMEM)
    vmem = pl.BlockSpec(memory_space=pltpu.VMEM)
    return pl.pallas_call(
        functools.partial(rotation_kernel, which),
        in_specs=[smem, smem, vmem, vmem],
        out_specs=[vmem, vmem],
        out_shape=[jax.ShapeDtypeStruct((2 * width, 2 * width), BF16)] * 2,
        compiler_params=params(8),
    )(flags, offsets, one, two)


def first_product_kernel(
    early, flags_ref, x_ref, a_ref, b_ref, u1_ref, w1_ref, u2_ref, w2_ref, sent_ref
):
    ya = times(x_ref[0], a_ref[...])
    yb = times(x_ref[1], b_ref[...])
    left = left_lanes(ya.shape)
    up = jnp.where(left, ya, yb)
    down = jnp.where(left, yb, ya)
    sent_ref[...] = jnp.where(flags_ref[2] == 1, down, up)
    step = pl.program_id(0)

    @pl.when(step < early)
    def _():
        u1_ref[...] = up
        w1_ref[...] = down

    @pl.when(step >= early)
    def _():
        u2_ref[...] = up
        w2_ref[...] = down


def first_product(flags, x, a, b, block, early):
    _, rows, width = x.shape
    steps = rows // block
    whole = pl.BlockSpec(a.shape, lambda i, f: (0, 0))
    one = pl.BlockSpec((block, width), lambda i, f: (jnp.minimum(i, early - 1), 0))
    two = pl.BlockSpec((block, width), lambda i, f: (jnp.maximum(i - early, 0), 0))
    shape_one = jax.ShapeDtypeStruct((early * block, width), F32)
    shape_two = jax.ShapeDtypeStruct((rows - early * block, width), F32)
    return pl.pallas_call(
        functools.partial(first_product_kernel, early),
        grid_spec=pltpu.PrefetchScalarGridSpec(
            num_scalar_prefetch=1,
            grid=(steps,),
            in_specs=[
                pl.BlockSpec((2, block, width), lambda i, f: (0, i, 0)),
                whole,
                whole,
            ],
            out_specs=[one, one, two, two, pl.BlockSpec((block, width), lambda i, f: (i, 0))],
        ),
        out_shape=[
            shape_one,
            shape_one,
            shape_two,
            shape_two,
            jax.ShapeDtypeStruct((rows, width), F32),
        ],
        compiler_params=params(),
    )(flags, x, a, b)


def pair_gram_kernel(
    early, flags_ref, got_ref, u1_ref, w1_ref, u2_ref, w2_ref, gram_ref, a_ref, b_ref
):
    step = pl.program_id(0)

    @pl.when(step == 0)
    def _():
        a_ref[...] = jnp.zeros_like(a_ref)
        b_ref[...] = jnp.zeros_like(b_ref)

    def add(u_ref, w_ref):
        own = jnp.where(flags_ref[2] == 1, u_ref[...], w_ref[...])
        at_end = flags_ref[0] + flags_ref[1]
        own = jnp.where(at_end == 1, swapped(own, 1), own)
        got = got_ref[...]
        first = jnp.where(flags_ref[3] == 1, own, got)
        second = jnp.where(flags_ref[3] == 1, got, own)
        left = left_lanes(got.shape)
        a_ref[...] += gram_terms(jnp.where(left, first, second))
        b_ref[...] += gram_terms(jnp.where(left, second, first))

    @pl.when(step < early)
    def _():
        add(u1_ref, w1_ref)

    @pl.when(step >= early)
    def _():
        add(u2_ref, w2_ref)

    @pl.when(step == pl.num_programs(0) - 1)
    def _():
        other = gram_of_terms(b_ref[...])
        gram_ref[...] = gram_of_terms(a_ref[...]) + swapped(swapped(other, 0), 1)


def pair_gram(flags, got, u1, w1, u2, w2, block):
    rows, width = got.shape
    early = u1.shape[0] // block
    one = pl.BlockSpec((block, width), lambda i, f: (jnp.minimum(i, early - 1), 0))
    two = pl.BlockSpec((block, width), lambda i, f: (jnp.maximum(i - early, 0), 0))
    return pl.pallas_call(
        functools.partial(pair_gram_kernel, early),
        grid_spec=pltpu.PrefetchScalarGridSpec(
            num_scalar_prefetch=1,
            grid=(rows // block,),
            in_specs=[
                pl.BlockSpec((block, width), lambda i, f: (i, 0)),
                one,
                one,
                two,
                two,
            ],
            out_specs=pl.BlockSpec((width, width), lambda i, f: (0, 0)),
            scratch_shapes=[pltpu.VMEM((width, 2 * width), F32)] * 2,
        ),
        out_shape=jax.ShapeDtypeStruct((width, width), F32),
        compiler_params=params(),
    )(flags, got, u1, w1, u2, w2)


def second_product_kernel(
    flags_ref, up_ref, down_ref, got_ref, u_ref, w_ref, a_ref, b_ref, *rest
):
    out_ref = rest[-1]
    bottom = flags_ref[0] == 1
    top = flags_ref[1] == 1

    def finish(first, second):
        left = left_lanes(first.shape)
        out_ref[0] = times(jnp.where(left, first, second), a_ref[...])
        out_ref[1] = times(jnp.where(left, second, first), b_ref[...])

    @pl.when(jnp.logical_not(jnp.logical_or(bottom, top)))
    def _():
        finish(up_ref[...], down_ref[...])

    @pl.when(bottom)
    def _():
        finish(swapped(w_ref[...], 1), got_ref[...])

    @pl.when(top)
    def _():
        finish(got_ref[...], swapped(u_ref[...], 1))


def second_product(flags, up, down, got, u, w, a, b, out, start, total, block):
    rows, width = up.shape
    first = start // block
    rows_spec = pl.BlockSpec((block, width), lambda i, f: (i, 0))
    kept = pl.BlockSpec((block, width), lambda i, f: (i * (f[0] + f[1]), 0))
    got_spec = pl.BlockSpec((block, width), lambda i, f: ((i + first) * (f[0] + f[1]), 0))
    whole = pl.BlockSpec(a.shape, lambda i, f: (0, 0))
    operands = [flags, up, down, got, u, w, a, b]
    in_specs = [rows_spec, rows_spec, got_spec, kept, kept, whole, whole]
    aliases = {}
    if out is not None:
        aliases = {len(operands): 0}
        operands.append(out)
        in_specs.append(pl.BlockSpec(memory_space=pl.ANY))
    return pl.pallas_call(
        second_product_kernel,
        grid_spec=pltpu.PrefetchScalarGridSpec(
            num_scalar_prefetch=1,
            grid=(rows // block,),
            in_specs=in_specs,
            out_specs=pl.BlockSpec((2, block, width), lambda i, f: (0, i + first, 0)),
        ),
        out_shape=jax.ShapeDtypeStruct((2, total, width), F32),
        input_output_aliases=aliases,
        compiler_params=params(),
    )(*operands)


def row_partner(x, bit):
    size = lax.axis_size("rows")
    return lax.ppermute(x, "rows", [(i, i ^ bit) for i in range(size)])


def body(block, x, offsets):
    rows, width = x.shape
    half_rows = rows // 2
    steps = half_rows // block
    early = steps - 1
    place = lax.axis_index("loop")
    count = lax.axis_size("loop")
    last = count - 1
    odd = place % 2
    flags = jnp.stack(
        [
            (place == 0).astype(jnp.int32),
            (place == last).astype(jnp.int32),
            odd.astype(jnp.int32),
            ((place == 0) | ((odd == 1) & (place != last))).astype(jnp.int32),
        ]
    )
    halves = x.reshape(2, half_rows, width)

    gram = local_gram(x, 2 * block)
    gram = gram + row_partner(gram, 1)
    a, b = rotations(0, flags, offsets, gram, row_partner(gram, 2))
    u1, w1, u2, w2, sent = first_product(flags, halves, a, b, block, early)

    ups = [(i, i + 1) for i in range(last - 1)]
    downs = [(i, i - 1) for i in range(2, count)]
    skips = (
        [(i, i + 2) for i in range(0, last - 1, 2)]
        + [(i, i - 2) for i in range(3, count, 2)]
        + [(1, 0), (last - 1, last)]
    )
    homes = (
        [(i, i - 1) for i in range(2, count, 2)]
        + [(i, i + 1) for i in range(1, last, 2)]
        + [(0, 0), (last, last)]
    )
    up1 = lax.ppermute(u1, "loop", ups)
    down1 = lax.ppermute(w1, "loop", downs)
    got = lax.ppermute(sent, "loop", skips)
    up2 = lax.ppermute(u2, "loop", ups)
    down2 = lax.ppermute(w2, "loop", downs)

    gram = pair_gram(flags, got, u1, w1, u2, w2, block)
    gram = lax.ppermute(gram, "loop", homes)
    gram = gram + row_partner(gram, 1)
    a, b = rotations(1, flags, offsets, gram, row_partner(gram, 2))

    out = second_product(flags, up1, down1, got, u1, w1, a, b, None, 0, half_rows, block)
    out = second_product(
        flags, up2, down2, got, u2, w2, a, b, out, early * block, half_rows, block
    )
    return out.reshape(rows, width)


def solution(mesh, block=1024):
    placed = (P("rows", "loop"), P())
    return jax.shard_map(
        functools.partial(body, block),
        mesh=mesh,
        in_specs=placed,
        out_specs=P("rows", "loop"),
        check_vma=False,
    )
```

```python
import functools

import jax
import jax.numpy as jnp
from jax import lax
from jax.experimental import pallas as pl
from jax.experimental.pallas import tpu as pltpu
from jax.sharding import PartitionSpec as P

ROUNDS = 4
MIB = 1024 * 1024
F32 = jnp.float32
BF16 = jnp.bfloat16


def params(mib=58):
    return pltpu.CompilerParams(vmem_limit_bytes=mib * MIB)


def parts(x):
    high = x.astype(BF16)
    low = (x - high.astype(F32)).astype(BF16)
    return high, low


def gram_terms(x):
    high, low = parts(x)
    return lax.dot_general(
        high,
        jnp.concatenate([high, low], axis=1),
        (((0,), (0,)), ((), ())),
        preferred_element_type=F32,
    )


def gram_of_terms(terms):
    width = terms.shape[0]
    cross = terms[:, width:]
    return terms[:, :width] + cross + cross.T


def swapped(x, axis):
    return pltpu.roll(x, x.shape[axis] // 2, axis)


def times(x, weights):
    width = x.shape[1]
    both = jnp.dot(
        jnp.concatenate(parts(x), axis=1), weights, preferred_element_type=F32
    )
    return both[:, :width] + both[:, width:]


def left_lanes(shape):
    return lax.broadcasted_iota(jnp.int32, shape, 1) < shape[1] // 2


def gram_kernel(x_ref, gram_ref, terms_ref):
    step = pl.program_id(0)

    @pl.when(step == 0)
    def _():
        terms_ref[...] = jnp.zeros_like(terms_ref)

    terms_ref[...] += gram_terms(x_ref[...])

    @pl.when(step == pl.num_programs(0) - 1)
    def _():
        gram_ref[...] = gram_of_terms(terms_ref[...])


def local_gram(x, block):
    rows, width = x.shape
    return pl.pallas_call(
        gram_kernel,
        grid=(rows // block,),
        in_specs=[pl.BlockSpec((block, width), lambda i: (i, 0))],
        out_specs=pl.BlockSpec((width, width), lambda i: (0, 0)),
        out_shape=jax.ShapeDtypeStruct((width, width), F32),
        scratch_shapes=[pltpu.VMEM((width, 2 * width), F32)],
        compiler_params=params(),
    )(x)


def rotation_kernel(which, flags_ref, offsets_ref, one_ref, two_ref, a_ref, b_ref):
    gram = one_ref[...] + two_ref[...]
    width = gram.shape[0]
    half = width // 2
    row = lax.broadcasted_iota(jnp.int32, (width, width), 0)
    lane = lax.broadcasted_iota(jnp.int32, (width, width), 1)
    eye = row == lane
    is_first = lax.broadcasted_iota(jnp.int32, (1, width), 1) < half
    vectors = jnp.where(eye, 1.0, 0.0).astype(F32)
    dot = functools.partial(
        jnp.dot, precision=lax.Precision.HIGHEST, preferred_element_type=F32
    )
    for turn in range(ROUNDS):
        offset = offsets_ref[which, turn]
        above = lane + offset
        above = half + jnp.where(above >= half, above - half, above)
        below = lane - half - offset
        below = jnp.where(below < 0, below + half, below)
        pair = row == jnp.where(lane < half, above, below)
        own = jnp.sum(jnp.where(eye, gram, 0.0), axis=0, keepdims=True)
        own_col = jnp.sum(jnp.where(eye, gram, 0.0), axis=1, keepdims=True)
        other = jnp.sum(jnp.where(pair, own_col, 0.0), axis=0, keepdims=True)
        cross = jnp.sum(jnp.where(pair, gram, 0.0), axis=0, keepdims=True)
        spread = jnp.where(is_first, other - own, own - other)
        sign = jnp.where(spread >= 0.0, 1.0, -1.0)
        tangent = (
            sign
            * 2.0
            * cross
            / (jnp.abs(spread) + jnp.sqrt(spread * spread + 4.0 * cross * cross))
        )
        cosine = 1.0 / jnp.sqrt(1.0 + tangent * tangent)
        sine = tangent * cosine
        signed = jnp.where(is_first, -sine, sine)
        on_diagonal = jnp.where(eye, cosine, 0.0)
        off_diagonal = jnp.where(pair, signed, 0.0)
        turned = on_diagonal + off_diagonal
        vectors = dot(vectors, turned)
        if turn < ROUNDS - 1:
            gram = dot(on_diagonal - off_diagonal, dot(gram, turned))
    if which == 0:
        vectors = jnp.where(flags_ref[0] == 1, swapped(vectors, 1), vectors)
        other_vectors = swapped(vectors, 1)
    else:
        other_vectors = swapped(vectors, 0)
    for out_ref, v in ((a_ref, vectors), (b_ref, other_vectors)):
        both = jnp.concatenate(parts(v), axis=1)
        out_ref[...] = jnp.concatenate([both, both], axis=0)


def rotations(which, flags, offsets, one, two):
    width = one.shape[0]
    smem = pl.BlockSpec(memory_space=pltpu.SMEM)
    vmem = pl.BlockSpec(memory_space=pltpu.VMEM)
    return pl.pallas_call(
        functools.partial(rotation_kernel, which),
        in_specs=[smem, smem, vmem, vmem],
        out_specs=[vmem, vmem],
        out_shape=[jax.ShapeDtypeStruct((2 * width, 2 * width), BF16)] * 2,
        compiler_params=params(8),
    )(flags, offsets, one, two)


def run_spec(low, count, block, width):
    return pl.BlockSpec(
        (block, width), lambda i, f: (jnp.clip(i - low, 0, count - 1), 0)
    )


def first_product_kernel(runs, flags_ref, x_ref, a_ref, b_ref, *out_refs):
    ya = times(x_ref[0], a_ref[...])
    yb = times(x_ref[1], b_ref[...])
    left = left_lanes(ya.shape)
    up = jnp.where(left, ya, yb)
    down = jnp.where(left, yb, ya)
    step = pl.program_id(0)
    for which, (low, count) in enumerate(runs):

        @pl.when((step >= low) & (step < low + count))
        def _():
            out_refs[2 * which][...] = up
            out_refs[2 * which + 1][...] = down

    @pl.when(step >= runs[0][1])
    def _():
        out_refs[-1][...] = jnp.where(flags_ref[2] == 1, down, up)


def first_product(flags, x, a, b, block, runs):
    _, rows, width = x.shape
    steps = rows // block
    first_run = runs[0][1]
    whole = pl.BlockSpec(a.shape, lambda i, f: (0, 0))
    out_specs, out_shape = [], []
    for low, count in runs + [(first_run, steps - first_run)]:
        for _ in range(2 if len(out_specs) < 2 * len(runs) else 1):
            out_specs.append(run_spec(low, count, block, width))
            out_shape.append(jax.ShapeDtypeStruct((count * block, width), F32))
    return pl.pallas_call(
        functools.partial(first_product_kernel, runs),
        grid_spec=pltpu.PrefetchScalarGridSpec(
            num_scalar_prefetch=1,
            grid=(steps,),
            in_specs=[
                pl.BlockSpec((2, block, width), lambda i, f: (0, i, 0)),
                whole,
                whole,
            ],
            out_specs=out_specs,
        ),
        out_shape=out_shape,
        compiler_params=params(),
    )(flags, x, a, b)


def packed_gram_kernel(halves, flags_ref, *refs):
    *in_refs, gram_ref, a_ref, b_ref = refs
    step = pl.program_id(0)

    @pl.when(step == 0)
    def _():
        a_ref[...] = jnp.zeros_like(a_ref)
        b_ref[...] = jnp.zeros_like(b_ref)

    def add(first, second):
        left = left_lanes(first.shape)
        a_ref[...] += gram_terms(jnp.where(left, first, second))
        b_ref[...] += gram_terms(jnp.where(left, second, first))

    halves(step, flags_ref, add, *in_refs)

    @pl.when(step == pl.num_programs(0) - 1)
    def _():
        other = gram_of_terms(b_ref[...])
        gram_ref[...] = gram_of_terms(a_ref[...]) + swapped(swapped(other, 0), 1)


def neighbour_halves(early, step, flags_ref, add, got_ref, *own_refs):
    def with_own(u_ref, w_ref):
        own = jnp.where(flags_ref[2] == 1, u_ref[...], w_ref[...])
        at_end = flags_ref[0] + flags_ref[1]
        own = jnp.where(at_end == 1, swapped(own, 1), own)
        got = got_ref[...]
        own_first = flags_ref[3] == 1
        add(jnp.where(own_first, own, got), jnp.where(own_first, got, own))

    @pl.when(step < early)
    def _():
        with_own(*own_refs[:2])

    @pl.when(step >= early)
    def _():
        with_own(*own_refs[2:])


def arrived_halves(step, flags_ref, add, up_ref, down_ref, u_ref, w_ref):
    bottom = flags_ref[0] == 1
    top = flags_ref[1] == 1

    @pl.when(jnp.logical_not(jnp.logical_or(bottom, top)))
    def _():
        add(up_ref[...], down_ref[...])

    @pl.when(bottom)
    def _():
        add(swapped(w_ref[...], 1), down_ref[...])

    @pl.when(top)
    def _():
        add(up_ref[...], swapped(u_ref[...], 1))


def skipped_halves(step, flags_ref, add, up_ref, down_ref, u_ref, w_ref, got_ref):
    bottom = flags_ref[0] == 1
    top = flags_ref[1] == 1

    @pl.when(jnp.logical_not(jnp.logical_or(bottom, top)))
    def _():
        add(up_ref[...], down_ref[...])

    @pl.when(bottom)
    def _():
        add(swapped(w_ref[...], 1), got_ref[...])

    @pl.when(top)
    def _():
        add(got_ref[...], swapped(u_ref[...], 1))


def gram_call(halves, flags, operands, specs, steps):
    width = operands[0].shape[1]
    return pl.pallas_call(
        functools.partial(packed_gram_kernel, halves),
        grid_spec=pltpu.PrefetchScalarGridSpec(
            num_scalar_prefetch=1,
            grid=(steps,),
            in_specs=specs,
            out_specs=pl.BlockSpec((width, width), lambda i, f: (0, 0)),
            scratch_shapes=[pltpu.VMEM((width, 2 * width), F32)] * 2,
        ),
        out_shape=jax.ShapeDtypeStruct((width, width), F32),
        compiler_params=params(),
    )(flags, *operands)


def neighbour_gram(flags, got, u2, w2, u3, w3, block):
    rows, width = got.shape
    early = u2.shape[0] // block
    late = u3.shape[0] // block
    one = run_spec(0, early, block, width)
    two = run_spec(early, late, block, width)
    every = run_spec(0, early + late, block, width)
    return gram_call(
        functools.partial(neighbour_halves, early),
        flags,
        [got, u2, w2, u3, w3],
        [every, one, one, two, two],
        early + late,
    )


def kept_spec(block, width):
    return pl.BlockSpec((block, width), lambda i, f: (i * (f[0] + f[1]), 0))


def arrived_gram(flags, up, down, u, w, block):
    rows, width = up.shape
    steps = rows // block
    every = run_spec(0, steps, block, width)
    kept = kept_spec(block, width)
    return gram_call(
        arrived_halves, flags, [up, down, u, w], [every, every, kept, kept], steps
    )


def second_product_kernel(halves, count, flags_ref, a_ref, b_ref, *refs):
    out_ref = refs[-1]

    def finish(first, second):
        left = left_lanes(first.shape)
        out_ref[0] = times(jnp.where(left, first, second), a_ref[...])
        out_ref[1] = times(jnp.where(left, second, first), b_ref[...])

    halves(pl.program_id(0), flags_ref, finish, *refs[:count])


def second_product(flags, a, b, operands, got, got_start, out, start, total, block):
    rows, width = operands[0].shape
    first = start // block
    got_first = got_start // block
    every = run_spec(0, rows // block, block, width)
    kept = kept_spec(block, width)
    whole = pl.BlockSpec(a.shape, lambda i, f: (0, 0))
    in_specs = [whole, whole, every, every, kept, kept]
    operands = list(operands)
    halves = arrived_halves
    if got is not None:
        halves = skipped_halves
        operands.append(got)
        in_specs.append(
            pl.BlockSpec(
                (block, width), lambda i, f: ((i + got_first) * (f[0] + f[1]), 0)
            )
        )
    count = len(operands)
    aliases = {}
    if out is not None:
        aliases = {3 + count: 0}
        operands.append(out)
        in_specs.append(pl.BlockSpec(memory_space=pl.ANY))
    return pl.pallas_call(
        functools.partial(second_product_kernel, halves, count),
        grid_spec=pltpu.PrefetchScalarGridSpec(
            num_scalar_prefetch=1,
            grid=(rows // block,),
            in_specs=in_specs,
            out_specs=pl.BlockSpec((2, block, width), lambda i, f: (0, i + first, 0)),
        ),
        out_shape=jax.ShapeDtypeStruct((2, total, width), F32),
        input_output_aliases=aliases,
        compiler_params=params(),
    )(flags, a, b, *operands)


def row_partner(x, bit):
    size = lax.axis_size("rows")
    return lax.ppermute(x, "rows", [(i, i ^ bit) for i in range(size)])


def body(block, x, offsets):
    rows, width = x.shape
    half_rows = rows // 2
    steps = half_rows // block
    late = max(1, steps // 12)
    middle = max(1, steps // 4)
    runs = [
        (0, steps - middle - late),
        (steps - middle - late, middle),
        (steps - late, late),
    ]
    place = lax.axis_index("loop")
    count = lax.axis_size("loop")
    last = count - 1
    odd = place % 2
    flags = jnp.stack(
        [
            (place == 0).astype(jnp.int32),
            (place == last).astype(jnp.int32),
            odd.astype(jnp.int32),
            ((place == 0) | ((odd == 1) & (place != last))).astype(jnp.int32),
        ]
    )
    halves = x.reshape(2, half_rows, width)

    gram = local_gram(x, 2 * block)
    gram = gram + row_partner(gram, 1)
    a, b = rotations(0, flags, offsets, gram, row_partner(gram, 2))
    u1, w1, u2, w2, u3, w3, sent = first_product(flags, halves, a, b, block, runs)

    ups = [(i, i + 1) for i in range(last)]
    downs = [(i, i - 1) for i in range(1, count)]
    skips = (
        [(i, i + 2) for i in range(0, last - 1, 2)]
        + [(i, i - 2) for i in range(3, count, 2)]
        + [(1, 0), (last - 1, last)]
    )
    homes = (
        [(i, i - 1) for i in range(2, count, 2)]
        + [(i, i + 1) for i in range(1, last, 2)]
        + [(0, 0), (last, last)]
    )
    up1 = lax.ppermute(u1, "loop", ups)
    down1 = lax.ppermute(w1, "loop", downs)
    got = lax.ppermute(sent, "loop", skips)
    up2 = lax.ppermute(u2, "loop", ups[:-1])
    down2 = lax.ppermute(w2, "loop", downs[1:])
    up3 = lax.ppermute(u3, "loop", ups[:-1])
    down3 = lax.ppermute(w3, "loop", downs[1:])

    gram = neighbour_gram(flags, got, u2, w2, u3, w3, block)
    gram = lax.ppermute(gram, "loop", homes)
    gram = gram + arrived_gram(flags, up1, down1, u1, w1, block)
    gram = gram + row_partner(gram, 1)
    a, b = rotations(1, flags, offsets, gram, row_partner(gram, 2))

    out = None
    for (low, _), arrays, got_start, size in (
        (runs[0], (up1, down1, u1, w1), None, block),
        (runs[1], (up2, down2, u2, w2), 0, block),
        (runs[2], (up3, down3, u3, w3), runs[1][1] * block, max(16, block // 4)),
    ):
        out = second_product(
            flags,
            a,
            b,
            arrays,
            None if got_start is None else got,
            got_start or 0,
            out,
            low * block,
            half_rows,
            size,
        )
    return out.reshape(rows, width)


def solution(mesh, block=1024):
    placed = (P("rows", "loop"), P())
    return jax.shard_map(
        functools.partial(body, block),
        mesh=mesh,
        in_specs=placed,
        out_specs=P("rows", "loop"),
        check_vma=False,
    )
```

```python
import functools

import jax
import jax.numpy as jnp
from jax import lax
from jax.experimental import pallas as pl
from jax.experimental.pallas import tpu as pltpu
from jax.sharding import PartitionSpec as P

ROUNDS = 4
MIB = 1024 * 1024
F32 = jnp.float32
BF16 = jnp.bfloat16
HINT = pl.CostEstimate(flops=1000, bytes_accessed=1000, transcendentals=0)


def params(mib=58):
    return pltpu.CompilerParams(vmem_limit_bytes=mib * MIB)


def parts(x):
    high = x.astype(BF16)
    low = (x - high.astype(F32)).astype(BF16)
    return high, low


def gram_terms(x):
    high, low = parts(x)
    return lax.dot_general(
        high,
        jnp.concatenate([high, low], axis=1),
        (((0,), (0,)), ((), ())),
        preferred_element_type=F32,
    )


def gram_of_terms(terms):
    width = terms.shape[0]
    cross = terms[:, width:]
    return terms[:, :width] + cross + cross.T


def swapped(x, axis):
    return pltpu.roll(x, x.shape[axis] // 2, axis)


def times(x, weights):
    width = x.shape[1]
    both = jnp.dot(
        jnp.concatenate(parts(x), axis=1), weights, preferred_element_type=F32
    )
    return both[:, :width] + both[:, width:]


def weights_of(v):
    both = jnp.concatenate(parts(v), axis=1)
    return jnp.concatenate([both, both], axis=0)


def left_lanes(shape):
    return lax.broadcasted_iota(jnp.int32, shape, 1) < shape[1] // 2


def gram_kernel(x_ref, gram_ref, terms_ref):
    step = pl.program_id(0)

    @pl.when(step == 0)
    def _():
        terms_ref[...] = jnp.zeros_like(terms_ref)

    terms_ref[...] += gram_terms(x_ref[...])

    @pl.when(step == pl.num_programs(0) - 1)
    def _():
        gram_ref[...] = gram_of_terms(terms_ref[...])


def local_gram(x, block):
    rows, width = x.shape
    return pl.pallas_call(
        gram_kernel,
        grid=(rows // block,),
        in_specs=[pl.BlockSpec((block, width), lambda i: (i, 0))],
        out_specs=pl.BlockSpec((width, width), lambda i: (0, 0)),
        out_shape=jax.ShapeDtypeStruct((width, width), F32),
        scratch_shapes=[pltpu.VMEM((width, 2 * width), F32)],
        cost_estimate=HINT,
        compiler_params=params(),
    )(x)


def rotation_kernel(which, flags_ref, offsets_ref, one_ref, two_ref, a_ref, b_ref, v_ref):
    gram = one_ref[...] + two_ref[...]
    width = gram.shape[0]
    half = width // 2
    row = lax.broadcasted_iota(jnp.int32, (width, width), 0)
    lane = lax.broadcasted_iota(jnp.int32, (width, width), 1)
    eye = row == lane
    is_first = lax.broadcasted_iota(jnp.int32, (1, width), 1) < half
    vectors = jnp.where(eye, 1.0, 0.0).astype(F32)
    dot = functools.partial(
        jnp.dot, precision=lax.Precision.HIGHEST, preferred_element_type=F32
    )
    for turn in range(ROUNDS):
        offset = offsets_ref[which, turn]
        above = lane + offset
        above = half + jnp.where(above >= half, above - half, above)
        below = lane - half - offset
        below = jnp.where(below < 0, below + half, below)
        pair = row == jnp.where(lane < half, above, below)
        own = jnp.sum(jnp.where(eye, gram, 0.0), axis=0, keepdims=True)
        own_col = jnp.sum(jnp.where(eye, gram, 0.0), axis=1, keepdims=True)
        other = jnp.sum(jnp.where(pair, own_col, 0.0), axis=0, keepdims=True)
        cross = jnp.sum(jnp.where(pair, gram, 0.0), axis=0, keepdims=True)
        spread = jnp.where(is_first, other - own, own - other)
        sign = jnp.where(spread >= 0.0, 1.0, -1.0)
        tangent = (
            sign
            * 2.0
            * cross
            / (jnp.abs(spread) + jnp.sqrt(spread * spread + 4.0 * cross * cross))
        )
        cosine = 1.0 / jnp.sqrt(1.0 + tangent * tangent)
        sine = tangent * cosine
        signed = jnp.where(is_first, -sine, sine)
        on_diagonal = jnp.where(eye, cosine, 0.0)
        off_diagonal = jnp.where(pair, signed, 0.0)
        turned = on_diagonal + off_diagonal
        vectors = dot(vectors, turned)
        if turn < ROUNDS - 1:
            gram = dot(on_diagonal - off_diagonal, dot(gram, turned))
    if which == 0:
        vectors = jnp.where(flags_ref[0] == 1, swapped(vectors, 1), vectors)
        other_vectors = swapped(vectors, 1)
    else:
        other_vectors = swapped(vectors, 0)
    v_ref[...] = vectors
    a_ref[...] = weights_of(vectors)
    b_ref[...] = weights_of(other_vectors)


def rotations(which, flags, offsets, one, two):
    width = one.shape[0]
    smem = pl.BlockSpec(memory_space=pltpu.SMEM)
    vmem = pl.BlockSpec(memory_space=pltpu.VMEM)
    return pl.pallas_call(
        functools.partial(rotation_kernel, which),
        in_specs=[smem, smem, vmem, vmem],
        out_specs=[vmem, vmem, vmem],
        out_shape=[jax.ShapeDtypeStruct((2 * width, 2 * width), BF16)] * 2
        + [jax.ShapeDtypeStruct((width, width), F32)],
        cost_estimate=HINT,
        compiler_params=params(8),
    )(flags, offsets, one, two)


def run_spec(low, count, block, width):
    return pl.BlockSpec(
        (block, width), lambda i, f: (jnp.clip(i - low, 0, count - 1), 0)
    )


def first_product_kernel(runs, skip, flags_ref, x_ref, a_ref, b_ref, *out_refs):
    ya = times(x_ref[0], a_ref[...])
    yb = times(x_ref[1], b_ref[...])
    left = left_lanes(ya.shape)
    up = jnp.where(left, ya, yb)
    down = jnp.where(left, yb, ya)
    step = pl.program_id(0)
    for which, (low, count) in enumerate(runs):

        @pl.when((step >= low) & (step < low + count))
        def _():
            out_refs[2 * which][...] = up
            out_refs[2 * which + 1][...] = down

    if skip:
        out_refs[2 * len(runs)][...] = jnp.where(flags_ref[2] == 1, down, up)


def first_product(flags, x, a, b, start, block, runs, skip):
    width = x.shape[2]
    steps = sum(count for _, count in runs)
    first = start // block
    whole = pl.BlockSpec(a.shape, lambda i, f: (0, 0))
    out_specs, out_shape = [], []
    for low, count in [run for run in runs for _ in range(2)] + [(0, steps)] * skip:
        out_specs.append(run_spec(low, count, block, width))
        out_shape.append(jax.ShapeDtypeStruct((count * block, width), F32))
    return pl.pallas_call(
        functools.partial(first_product_kernel, runs, skip),
        grid_spec=pltpu.PrefetchScalarGridSpec(
            num_scalar_prefetch=1,
            grid=(steps,),
            in_specs=[
                pl.BlockSpec((2, block, width), lambda i, f: (0, i + first, 0)),
                whole,
                whole,
            ],
            out_specs=out_specs,
        ),
        out_shape=out_shape,
        cost_estimate=HINT,
        compiler_params=params(),
    )(flags, x, a, b)


def gated_kernel(count, *refs):
    refs[count][...] = refs[0][...]


def gate(v, arrived, passed):
    anywhere = pl.BlockSpec(memory_space=pl.ANY)
    vmem = pl.BlockSpec(memory_space=pltpu.VMEM)
    low = 1 + len(arrived)
    return pl.pallas_call(
        functools.partial(gated_kernel, low + len(passed)),
        in_specs=[vmem] + [anywhere] * (len(arrived) + len(passed)),
        out_specs=[vmem] + [anywhere] * len(passed),
        out_shape=[jax.ShapeDtypeStruct(p.shape, p.dtype) for p in (v, *passed)],
        input_output_aliases={low + k: 1 + k for k in range(len(passed))},
        cost_estimate=HINT,
        compiler_params=params(),
    )(v, *arrived, *passed)


def raw_pair_kernel(
    flags_ref,
    up_ref,
    down_ref,
    x_ref,
    v_up_ref,
    v_down_ref,
    v_ref,
    out_ref,
    gram_ref,
    terms_ref,
):
    step = pl.program_id(0)
    bottom = flags_ref[0] == 1
    top = flags_ref[1] == 1

    @pl.when(step == 0)
    def _():
        terms_ref[...] = jnp.zeros_like(terms_ref)

    own = swapped(v_ref[...], 1)
    left = left_lanes(own.shape)
    v_up = jnp.where(bottom, own, v_up_ref[...])
    v_down = jnp.where(top, own, v_down_ref[...])
    a = weights_of(jnp.where(left, v_up, 0.0))
    b = weights_of(jnp.where(left, 0.0, v_down))
    for side in range(2):
        x = x_ref[side]
        moved = times(jnp.where(bottom, x, up_ref[side]), a) + times(
            jnp.where(top, x, down_ref[side]), b
        )
        out_ref[side] = moved
        terms_ref[...] += gram_terms(moved)

    @pl.when(step == pl.num_programs(0) - 1)
    def _():
        gram_ref[...] = gram_of_terms(terms_ref[...])


def raw_pair(flags, up, down, x, start, v_up, v_down, v, block):
    _, rows, width = up.shape
    first = start // block
    every = pl.BlockSpec((2, block, width), lambda i, f: (0, i, 0))
    kept = pl.BlockSpec(
        (2, block, width), lambda i, f: (0, first + i * (f[0] + f[1]), 0)
    )
    square = pl.BlockSpec((width, width), lambda i, f: (0, 0))
    return pl.pallas_call(
        raw_pair_kernel,
        grid_spec=pltpu.PrefetchScalarGridSpec(
            num_scalar_prefetch=1,
            grid=(rows // block,),
            in_specs=[every, every, kept, square, square, square],
            out_specs=[every, square],
            scratch_shapes=[pltpu.VMEM((width, 2 * width), F32)],
        ),
        out_shape=[
            jax.ShapeDtypeStruct((2, rows, width), F32),
            jax.ShapeDtypeStruct((width, width), F32),
        ],
        cost_estimate=HINT,
        compiler_params=params(),
    )(flags, up, down, x, v_up, v_down, v)


def raw_product_kernel(x_ref, a_ref, out_ref):
    for side in range(2):
        out_ref[side] = times(x_ref[side], a_ref[...])


def raw_product(x, a, start, total, block):
    _, rows, width = x.shape
    first = start // block
    return pl.pallas_call(
        raw_product_kernel,
        grid=(rows // block,),
        in_specs=[
            pl.BlockSpec((2, block, width), lambda i: (0, i, 0)),
            pl.BlockSpec(a.shape, lambda i: (0, 0)),
        ],
        out_specs=pl.BlockSpec((2, block, width), lambda i: (0, i + first, 0)),
        out_shape=jax.ShapeDtypeStruct((2, total, width), F32),
        cost_estimate=HINT,
        compiler_params=params(),
    )(x, a)


def packed_gram_kernel(halves, flags_ref, *refs):
    *in_refs, gram_ref, a_ref, b_ref = refs
    step = pl.program_id(0)

    @pl.when(step == 0)
    def _():
        a_ref[...] = jnp.zeros_like(a_ref)
        b_ref[...] = jnp.zeros_like(b_ref)

    def add(first, second):
        left = left_lanes(first.shape)
        a_ref[...] += gram_terms(jnp.where(left, first, second))
        b_ref[...] += gram_terms(jnp.where(left, second, first))

    halves(step, flags_ref, add, *in_refs)

    @pl.when(step == pl.num_programs(0) - 1)
    def _():
        other = gram_of_terms(b_ref[...])
        gram_ref[...] = gram_of_terms(a_ref[...]) + swapped(swapped(other, 0), 1)


def neighbour_halves(early, step, flags_ref, add, got_ref, *own_refs):
    def with_own(u_ref, w_ref):
        own = jnp.where(flags_ref[2] == 1, u_ref[...], w_ref[...])
        at_end = flags_ref[0] + flags_ref[1]
        own = jnp.where(at_end == 1, swapped(own, 1), own)
        got = got_ref[...]
        own_first = flags_ref[3] == 1
        add(jnp.where(own_first, own, got), jnp.where(own_first, got, own))

    @pl.when(step < early)
    def _():
        with_own(*own_refs[:2])

    @pl.when(step >= early)
    def _():
        with_own(*own_refs[2:])


def arrived_halves(step, flags_ref, add, up_ref, down_ref, u_ref, w_ref):
    bottom = flags_ref[0] == 1
    top = flags_ref[1] == 1

    @pl.when(jnp.logical_not(jnp.logical_or(bottom, top)))
    def _():
        add(up_ref[...], down_ref[...])

    @pl.when(bottom)
    def _():
        add(swapped(w_ref[...], 1), down_ref[...])

    @pl.when(top)
    def _():
        add(up_ref[...], swapped(u_ref[...], 1))


def skipped_halves(step, flags_ref, add, up_ref, down_ref, u_ref, w_ref, got_ref):
    bottom = flags_ref[0] == 1
    top = flags_ref[1] == 1

    @pl.when(jnp.logical_not(jnp.logical_or(bottom, top)))
    def _():
        add(up_ref[...], down_ref[...])

    @pl.when(bottom)
    def _():
        add(swapped(w_ref[...], 1), got_ref[...])

    @pl.when(top)
    def _():
        add(got_ref[...], swapped(u_ref[...], 1))


def gram_call(halves, flags, operands, specs, steps):
    width = operands[0].shape[1]
    return pl.pallas_call(
        functools.partial(packed_gram_kernel, halves),
        grid_spec=pltpu.PrefetchScalarGridSpec(
            num_scalar_prefetch=1,
            grid=(steps,),
            in_specs=specs,
            out_specs=pl.BlockSpec((width, width), lambda i, f: (0, 0)),
            scratch_shapes=[pltpu.VMEM((width, 2 * width), F32)] * 2,
        ),
        out_shape=jax.ShapeDtypeStruct((width, width), F32),
        cost_estimate=HINT,
        compiler_params=params(),
    )(flags, *operands)


def neighbour_gram(flags, got, u2, w2, u3, w3, block):
    rows, width = got.shape
    early = u2.shape[0] // block
    late = u3.shape[0] // block
    one = run_spec(0, early, block, width)
    two = run_spec(early, late, block, width)
    every = run_spec(0, early + late, block, width)
    return gram_call(
        functools.partial(neighbour_halves, early),
        flags,
        [got, u2, w2, u3, w3],
        [every, one, one, two, two],
        early + late,
    )


def kept_spec(block, width):
    return pl.BlockSpec((block, width), lambda i, f: (i * (f[0] + f[1]), 0))


def arrived_gram(flags, up, down, u, w, block):
    rows, width = up.shape
    steps = rows // block
    every = run_spec(0, steps, block, width)
    kept = kept_spec(block, width)
    return gram_call(
        arrived_halves, flags, [up, down, u, w], [every, every, kept, kept], steps
    )


def second_product_kernel(halves, count, flags_ref, a_ref, b_ref, *refs):
    out_ref = refs[-1]

    def finish(first, second):
        left = left_lanes(first.shape)
        out_ref[0] = times(jnp.where(left, first, second), a_ref[...])
        out_ref[1] = times(jnp.where(left, second, first), b_ref[...])

    halves(pl.program_id(0), flags_ref, finish, *refs[:count])


def second_product(flags, a, b, operands, got, got_start, out, start, total, block):
    rows, width = operands[0].shape
    first = start // block
    got_first = got_start // block
    every = run_spec(0, rows // block, block, width)
    kept = kept_spec(block, width)
    whole = pl.BlockSpec(a.shape, lambda i, f: (0, 0))
    in_specs = [whole, whole, every, every, kept, kept]
    operands = list(operands)
    halves = arrived_halves
    if got is not None:
        halves = skipped_halves
        operands.append(got)
        in_specs.append(
            pl.BlockSpec(
                (block, width), lambda i, f: ((i + got_first) * (f[0] + f[1]), 0)
            )
        )
    count = len(operands)
    aliases = {}
    if out is not None:
        aliases = {3 + count: 0}
        operands.append(out)
        in_specs.append(pl.BlockSpec(memory_space=pl.ANY))
    return pl.pallas_call(
        functools.partial(second_product_kernel, halves, count),
        grid_spec=pltpu.PrefetchScalarGridSpec(
            num_scalar_prefetch=1,
            grid=(rows // block,),
            in_specs=in_specs,
            out_specs=pl.BlockSpec((2, block, width), lambda i, f: (0, i + first, 0)),
        ),
        out_shape=jax.ShapeDtypeStruct((2, total, width), F32),
        input_output_aliases=aliases,
        cost_estimate=HINT,
        compiler_params=params(),
    )(flags, a, b, *operands)


def row_partner(x, bit):
    size = lax.axis_size("rows")
    return lax.ppermute(x, "rows", [(i, i ^ bit) for i in range(size)])


def body(x, offsets):
    rows, width = x.shape
    half_rows = rows // 2
    unit = half_rows // 24
    first, middle, final, raw = 7 * unit, 14 * unit, 21 * unit, 22 * unit
    block = 7 * unit // 2
    place = lax.axis_index("loop")
    count = lax.axis_size("loop")
    last = count - 1
    odd = place % 2
    flags = jnp.stack(
        [
            (place == 0).astype(jnp.int32),
            (place == last).astype(jnp.int32),
            odd.astype(jnp.int32),
            ((place == 0) | ((odd == 1) & (place != last))).astype(jnp.int32),
        ]
    )
    halves = x.reshape(2, half_rows, width)

    ups = [(i, i + 1) for i in range(last)]
    downs = [(i, i - 1) for i in range(1, count)]
    skips = (
        [(i, i + 2) for i in range(0, last - 1, 2)]
        + [(i, i - 2) for i in range(3, count, 2)]
        + [(1, 0), (last - 1, last)]
    )
    homes = (
        [(i, i - 1) for i in range(2, count, 2)]
        + [(i, i + 1) for i in range(1, last, 2)]
        + [(0, 0), (last, last)]
    )

    bare = halves[:, raw:]
    raw_up = lax.ppermute(bare, "loop", ups)
    raw_down = lax.ppermute(bare, "loop", downs)

    gram = local_gram(x, rows // 3)
    gram = gram + row_partner(gram, 1)
    a, b, v = rotations(0, flags, offsets, gram, row_partner(gram, 2))

    *late, sent = first_product(
        flags, halves, a, b, middle, unit, [(0, 7), (7, 1)], True
    )
    early = first_product(flags, halves, a, b, 0, block, [(0, 2), (2, 2)], False)
    late_v, *sends = gate(v, [raw_up, raw_down], [*early, *late])
    u0, w0, u1, w1, u2, w2, u3, w3 = sends
    got = lax.ppermute(sent, "loop", skips)
    up0 = lax.ppermute(u0, "loop", ups)
    down0 = lax.ppermute(w0, "loop", downs)
    up1 = lax.ppermute(u1, "loop", ups)
    down1 = lax.ppermute(w1, "loop", downs)
    v_up = lax.ppermute(late_v, "loop", ups)
    v_down = lax.ppermute(late_v, "loop", downs)
    up2 = lax.ppermute(u2, "loop", ups[:-1])
    down2 = lax.ppermute(w2, "loop", downs[1:])
    up3 = lax.ppermute(u3, "loop", ups[:-1])
    down3 = lax.ppermute(w3, "loop", downs[1:])

    gram = neighbour_gram(flags, got, u2, w2, u3, w3, unit)
    gram = lax.ppermute(gram, "loop", homes)
    moved, raw_gram = raw_pair(
        flags, raw_up, raw_down, halves, raw, v_up, v_down, v, unit
    )
    gram = gram + raw_gram + arrived_gram(flags, up0, down0, u0, w0, block)
    gram = gram + arrived_gram(flags, up1, down1, u1, w1, block)
    gram = gram + row_partner(gram, 1)
    a, b, _ = rotations(1, flags, offsets, gram, row_partner(gram, 2))

    out = raw_product(moved, a, raw, half_rows, unit)
    for arrays, got_start, start, size in (
        ((up0, down0, u0, w0), None, 0, block),
        ((up1, down1, u1, w1), None, first, block),
        ((up2, down2, u2, w2), 0, middle, block),
        ((up3, down3, u3, w3), final - middle, final, unit),
    ):
        skipped = None if got_start is None else got
        out = second_product(
            flags, a, b, arrays, skipped, got_start or 0, out, start, half_rows, size
        )
    return out.reshape(rows, width)


def solution(mesh):
    placed = (P("rows", "loop"), P())
    return jax.shard_map(
        body,
        mesh=mesh,
        in_specs=placed,
        out_specs=P("rows", "loop"),
        check_vma=False,
    )
```

```python
import functools

import jax
import jax.numpy as jnp
from jax import lax
from jax.experimental import pallas as pl
from jax.experimental.pallas import tpu as pltpu
from jax.sharding import PartitionSpec as P

ROUNDS = 4
MIB = 1024 * 1024
F32 = jnp.float32
BF16 = jnp.bfloat16
HINT = pl.CostEstimate(flops=1000, bytes_accessed=1000, transcendentals=0)


def params(mib=58):
    return pltpu.CompilerParams(vmem_limit_bytes=mib * MIB)


def parts(x):
    high = x.astype(BF16)
    low = (x - high.astype(F32)).astype(BF16)
    return high, low


def gram_terms(x):
    high, low = parts(x)
    return lax.dot_general(
        high,
        jnp.concatenate([high, low], axis=1),
        (((0,), (0,)), ((), ())),
        preferred_element_type=F32,
    )


def gram_of_terms(terms):
    width = terms.shape[0]
    cross = terms[:, width:]
    return terms[:, :width] + cross + cross.T


def swapped(x, axis):
    return pltpu.roll(x, x.shape[axis] // 2, axis)


def times(x, weights):
    width = x.shape[1]
    both = jnp.dot(
        jnp.concatenate(parts(x), axis=1), weights, preferred_element_type=F32
    )
    return both[:, :width] + both[:, width:]


def weights_of(v):
    both = jnp.concatenate(parts(v), axis=1)
    return jnp.concatenate([both, both], axis=0)


def left_lanes(shape):
    return lax.broadcasted_iota(jnp.int32, shape, 1) < shape[1] // 2


def gram_kernel(x_ref, gram_ref, terms_ref):
    step = pl.program_id(0)

    @pl.when(step == 0)
    def _():
        terms_ref[...] = jnp.zeros_like(terms_ref)

    terms_ref[...] += gram_terms(x_ref[...])

    @pl.when(step == pl.num_programs(0) - 1)
    def _():
        gram_ref[...] = gram_of_terms(terms_ref[...])


def local_gram(x, block):
    rows, width = x.shape
    return pl.pallas_call(
        gram_kernel,
        grid=(rows // block,),
        in_specs=[pl.BlockSpec((block, width), lambda i: (i, 0))],
        out_specs=pl.BlockSpec((width, width), lambda i: (0, 0)),
        out_shape=jax.ShapeDtypeStruct((width, width), F32),
        scratch_shapes=[pltpu.VMEM((width, 2 * width), F32)],
        cost_estimate=HINT,
        compiler_params=params(),
    )(x)


def rotation_kernel(which, flags_ref, offsets_ref, one_ref, two_ref, a_ref, b_ref):
    gram = one_ref[...] + two_ref[...]
    width = gram.shape[0]
    half = width // 2
    row = lax.broadcasted_iota(jnp.int32, (width, width), 0)
    lane = lax.broadcasted_iota(jnp.int32, (width, width), 1)
    eye = row == lane
    is_first = lax.broadcasted_iota(jnp.int32, (1, width), 1) < half
    vectors = jnp.where(eye, 1.0, 0.0).astype(F32)
    dot = functools.partial(
        jnp.dot, precision=lax.Precision.HIGHEST, preferred_element_type=F32
    )
    for turn in range(ROUNDS):
        offset = offsets_ref[which, turn]
        above = lane + offset
        above = half + jnp.where(above >= half, above - half, above)
        below = lane - half - offset
        below = jnp.where(below < 0, below + half, below)
        pair = row == jnp.where(lane < half, above, below)
        own = jnp.sum(jnp.where(eye, gram, 0.0), axis=0, keepdims=True)
        own_col = jnp.sum(jnp.where(eye, gram, 0.0), axis=1, keepdims=True)
        other = jnp.sum(jnp.where(pair, own_col, 0.0), axis=0, keepdims=True)
        cross = jnp.sum(jnp.where(pair, gram, 0.0), axis=0, keepdims=True)
        spread = jnp.where(is_first, other - own, own - other)
        sign = jnp.where(spread >= 0.0, 1.0, -1.0)
        tangent = (
            sign
            * 2.0
            * cross
            / (jnp.abs(spread) + jnp.sqrt(spread * spread + 4.0 * cross * cross))
        )
        cosine = 1.0 / jnp.sqrt(1.0 + tangent * tangent)
        sine = tangent * cosine
        signed = jnp.where(is_first, -sine, sine)
        on_diagonal = jnp.where(eye, cosine, 0.0)
        off_diagonal = jnp.where(pair, signed, 0.0)
        turned = on_diagonal + off_diagonal
        vectors = dot(vectors, turned)
        if turn < ROUNDS - 1:
            gram = dot(on_diagonal - off_diagonal, dot(gram, turned))
    if which == 0:
        vectors = jnp.where(flags_ref[0] == 1, swapped(vectors, 1), vectors)
        other_vectors = swapped(vectors, 1)
    else:
        other_vectors = swapped(vectors, 0)
    a_ref[...] = weights_of(vectors)
    b_ref[...] = weights_of(other_vectors)


def rotations(which, flags, offsets, one, two):
    width = one.shape[0]
    smem = pl.BlockSpec(memory_space=pltpu.SMEM)
    vmem = pl.BlockSpec(memory_space=pltpu.VMEM)
    return pl.pallas_call(
        functools.partial(rotation_kernel, which),
        in_specs=[smem, smem, vmem, vmem],
        out_specs=[vmem, vmem],
        out_shape=[jax.ShapeDtypeStruct((2 * width, 2 * width), BF16)] * 2,
        cost_estimate=HINT,
        compiler_params=params(8),
    )(flags, offsets, one, two)


def run_spec(low, count, block, width):
    return pl.BlockSpec(
        (block, width), lambda i, f: (jnp.clip(i - low, 0, count - 1), 0)
    )


def first_product_kernel(runs, skip, flags_ref, x_ref, a_ref, b_ref, _, *out_refs):
    ya = times(x_ref[0], a_ref[...])
    yb = times(x_ref[1], b_ref[...])
    left = left_lanes(ya.shape)
    up = jnp.where(left, ya, yb)
    down = jnp.where(left, yb, ya)
    step = pl.program_id(0)
    for which, (low, count) in enumerate(runs):

        @pl.when((step >= low) & (step < low + count))
        def _():
            out_refs[2 * which][...] = up
            out_refs[2 * which + 1][...] = down

    if skip:
        out_refs[2 * len(runs)][...] = jnp.where(flags_ref[2] == 1, down, up)


def first_product(flags, x, a, b, earlier, start, block, runs, skip):
    width = x.shape[2]
    steps = sum(count for _, count in runs)
    first = start // block
    whole = pl.BlockSpec(a.shape, lambda i, f: (0, 0))
    out_specs, out_shape = [], []
    for low, count in [run for run in runs for _ in range(2)] + [(0, steps)] * skip:
        out_specs.append(run_spec(low, count, block, width))
        out_shape.append(jax.ShapeDtypeStruct((count * block, width), F32))
    return pl.pallas_call(
        functools.partial(first_product_kernel, runs, skip),
        grid_spec=pltpu.PrefetchScalarGridSpec(
            num_scalar_prefetch=1,
            grid=(steps,),
            in_specs=[
                pl.BlockSpec((2, block, width), lambda i, f: (0, i + first, 0)),
                whole,
                whole,
                pl.BlockSpec(memory_space=pl.ANY),
            ],
            out_specs=out_specs,
        ),
        out_shape=out_shape,
        cost_estimate=HINT,
        compiler_params=params(),
    )(flags, x, a, b, earlier)


def packed_gram_kernel(halves, flags_ref, *refs):
    *in_refs, gram_ref, a_ref, b_ref = refs
    step = pl.program_id(0)

    @pl.when(step == 0)
    def _():
        a_ref[...] = jnp.zeros_like(a_ref)
        b_ref[...] = jnp.zeros_like(b_ref)

    def add(first, second):
        left = left_lanes(first.shape)
        a_ref[...] += gram_terms(jnp.where(left, first, second))
        b_ref[...] += gram_terms(jnp.where(left, second, first))

    halves(step, flags_ref, add, *in_refs)

    @pl.when(step == pl.num_programs(0) - 1)
    def _():
        other = gram_of_terms(b_ref[...])
        gram_ref[...] = gram_of_terms(a_ref[...]) + swapped(swapped(other, 0), 1)


def neighbour_halves(early, step, flags_ref, add, got_ref, *own_refs):
    def with_own(u_ref, w_ref):
        own = jnp.where(flags_ref[2] == 1, u_ref[...], w_ref[...])
        at_end = flags_ref[0] + flags_ref[1]
        own = jnp.where(at_end == 1, swapped(own, 1), own)
        got = got_ref[...]
        own_first = flags_ref[3] == 1
        add(jnp.where(own_first, own, got), jnp.where(own_first, got, own))

    @pl.when(step < early)
    def _():
        with_own(*own_refs[:2])

    @pl.when(step >= early)
    def _():
        with_own(*own_refs[2:])


def arrived_halves(step, flags_ref, add, up_ref, down_ref, u_ref, w_ref):
    bottom = flags_ref[0] == 1
    top = flags_ref[1] == 1

    @pl.when(jnp.logical_not(jnp.logical_or(bottom, top)))
    def _():
        add(up_ref[...], down_ref[...])

    @pl.when(bottom)
    def _():
        add(swapped(w_ref[...], 1), down_ref[...])

    @pl.when(top)
    def _():
        add(up_ref[...], swapped(u_ref[...], 1))


def skipped_halves(step, flags_ref, add, up_ref, down_ref, u_ref, w_ref, got_ref):
    bottom = flags_ref[0] == 1
    top = flags_ref[1] == 1

    @pl.when(jnp.logical_not(jnp.logical_or(bottom, top)))
    def _():
        add(up_ref[...], down_ref[...])

    @pl.when(bottom)
    def _():
        add(swapped(w_ref[...], 1), got_ref[...])

    @pl.when(top)
    def _():
        add(got_ref[...], swapped(u_ref[...], 1))


def gram_call(halves, flags, operands, specs, steps):
    width = operands[0].shape[1]
    return pl.pallas_call(
        functools.partial(packed_gram_kernel, halves),
        grid_spec=pltpu.PrefetchScalarGridSpec(
            num_scalar_prefetch=1,
            grid=(steps,),
            in_specs=specs,
            out_specs=pl.BlockSpec((width, width), lambda i, f: (0, 0)),
            scratch_shapes=[pltpu.VMEM((width, 2 * width), F32)] * 2,
        ),
        out_shape=jax.ShapeDtypeStruct((width, width), F32),
        cost_estimate=HINT,
        compiler_params=params(),
    )(flags, *operands)


def neighbour_gram(flags, got, u2, w2, u3, w3, block):
    rows, width = got.shape
    early = u2.shape[0] // block
    late = u3.shape[0] // block
    one = run_spec(0, early, block, width)
    two = run_spec(early, late, block, width)
    every = run_spec(0, early + late, block, width)
    return gram_call(
        functools.partial(neighbour_halves, early),
        flags,
        [got, u2, w2, u3, w3],
        [every, one, one, two, two],
        early + late,
    )


def kept_spec(block, width):
    return pl.BlockSpec((block, width), lambda i, f: (i * (f[0] + f[1]), 0))


def arrived_gram(flags, up, down, u, w, block):
    rows, width = up.shape
    steps = rows // block
    every = run_spec(0, steps, block, width)
    kept = kept_spec(block, width)
    return gram_call(
        arrived_halves, flags, [up, down, u, w], [every, every, kept, kept], steps
    )


def second_product_kernel(halves, count, flags_ref, a_ref, b_ref, *refs):
    out_ref = refs[-1]

    def finish(first, second):
        left = left_lanes(first.shape)
        out_ref[0] = times(jnp.where(left, first, second), a_ref[...])
        out_ref[1] = times(jnp.where(left, second, first), b_ref[...])

    halves(pl.program_id(0), flags_ref, finish, *refs[:count])


def second_product(flags, a, b, operands, got, got_start, out, start, total, block):
    rows, width = operands[0].shape
    first = start // block
    got_first = got_start // block
    every = run_spec(0, rows // block, block, width)
    kept = kept_spec(block, width)
    whole = pl.BlockSpec(a.shape, lambda i, f: (0, 0))
    in_specs = [whole, whole, every, every, kept, kept]
    operands = list(operands)
    halves = arrived_halves
    if got is not None:
        halves = skipped_halves
        operands.append(got)
        in_specs.append(
            pl.BlockSpec(
                (block, width), lambda i, f: ((i + got_first) * (f[0] + f[1]), 0)
            )
        )
    count = len(operands)
    aliases = {}
    if out is not None:
        aliases = {3 + count: 0}
        operands.append(out)
        in_specs.append(pl.BlockSpec(memory_space=pl.ANY))
    return pl.pallas_call(
        functools.partial(second_product_kernel, halves, count),
        grid_spec=pltpu.PrefetchScalarGridSpec(
            num_scalar_prefetch=1,
            grid=(rows // block,),
            in_specs=in_specs,
            out_specs=pl.BlockSpec((2, block, width), lambda i, f: (0, i + first, 0)),
        ),
        out_shape=jax.ShapeDtypeStruct((2, total, width), F32),
        input_output_aliases=aliases,
        cost_estimate=HINT,
        compiler_params=params(),
    )(flags, a, b, *operands)


def row_partner(x, bit):
    size = lax.axis_size("rows")
    return lax.ppermute(x, "rows", [(i, i ^ bit) for i in range(size)])


def everywhere(x, target):
    rows, places = lax.axis_size("rows"), lax.axis_size("loop")
    pairs = []
    for row in range(rows):
        for place in range(places):
            where = target(row, place)
            pairs.append((row * places + place, where[0] * places + where[1]))
    return lax.ppermute(x, ("rows", "loop"), pairs)


def home(x, last):
    def onward(row, place):
        if place == 1:
            return row ^ 2, 0
        if place == last - 1:
            return row ^ 2, last
        return row, place - 2 if place % 2 else place + 2

    x = everywhere(x, lambda row, place: (row ^ 2, place ^ 1))
    return everywhere(x, onward)


def far_partner(x, count):
    ring = min(4, count // 2)

    def along(place):
        pair, odd = divmod(place, 2)
        group, at = divmod(pair, ring)
        at = (at - 1) % ring if odd else (at + 1) % ring
        return 2 * (group * ring + at) + odd

    x = everywhere(x, lambda row, place: (row ^ 2, along(place)))
    for _ in range(ring - 1):
        x = everywhere(x, lambda row, place: (row, along(place)))
    return x


def body(x, offsets):
    rows, width = x.shape
    half_rows = rows // 2
    small = half_rows // 12
    large = 5 * small // 2
    middle, late, final = 2 * large, 9 * small, 11 * small
    place = lax.axis_index("loop")
    count = lax.axis_size("loop")
    last = count - 1
    odd = place % 2
    flags = jnp.stack(
        [
            (place == 0).astype(jnp.int32),
            (place == last).astype(jnp.int32),
            odd.astype(jnp.int32),
            ((place == 0) | ((odd == 1) & (place != last))).astype(jnp.int32),
        ]
    )
    halves = x.reshape(2, half_rows, width)

    ups = [(i, i + 1) for i in range(last)]
    downs = [(i, i - 1) for i in range(1, count)]
    skips = (
        [(i, i + 2) for i in range(0, last - 1, 2)]
        + [(i, i - 2) for i in range(3, count, 2)]
        + [(1, 0), (last - 1, last)]
    )

    gram = local_gram(x, rows // 3)
    gram = gram + row_partner(gram, 1)
    a, b = rotations(0, flags, offsets, gram, row_partner(gram, 2))

    u2, w2, u3, w3, sent = first_product(
        flags, halves, a, b, halves, late, small, [(0, 2), (2, 1)], True
    )
    got = lax.ppermute(sent, "loop", skips)
    u0, w0 = first_product(flags, halves, a, b, sent, 0, large, [(0, 2)], False)
    up0 = lax.ppermute(u0, "loop", ups)
    down0 = lax.ppermute(w0, "loop", downs)
    u1, w1 = first_product(flags, halves, a, b, got, middle, small, [(0, 4)], False)
    up1 = lax.ppermute(u1, "loop", ups)
    down1 = lax.ppermute(w1, "loop", downs)
    up2 = lax.ppermute(u2, "loop", ups[:-1])
    down2 = lax.ppermute(w2, "loop", downs[1:])
    up3 = lax.ppermute(u3, "loop", ups[:-1])
    down3 = lax.ppermute(w3, "loop", downs[1:])

    gram = home(neighbour_gram(flags, got, u2, w2, u3, w3, small), last)
    gram = gram + arrived_gram(flags, up0, down0, u0, w0, large)
    gram = gram + arrived_gram(flags, up1, down1, u1, w1, small)
    gram = gram + row_partner(gram, 1)
    a, b = rotations(1, flags, offsets, gram, far_partner(gram, count))

    out = None
    for arrays, got_start, low, size in (
        ((up0, down0, u0, w0), None, 0, large),
        ((up1, down1, u1, w1), None, middle, small),
        ((up2, down2, u2, w2), 0, late, small),
        ((up3, down3, u3, w3), final - late, final, small),
    ):
        skipped = None if got_start is None else got
        out = second_product(
            flags, a, b, arrays, skipped, got_start or 0, out, low, half_rows, size
        )
    return out.reshape(rows, width)


def solution(mesh):
    placed = (P("rows", "loop"), P())
    return jax.shard_map(
        body,
        mesh=mesh,
        in_specs=placed,
        out_specs=P("rows", "loop"),
        check_vma=False,
    )
```

```python
import functools

import jax
import jax.numpy as jnp
from jax import lax
from jax.experimental import pallas as pl
from jax.experimental.pallas import tpu as pltpu
from jax.sharding import PartitionSpec as P

ROUNDS = 4
MIB = 1024 * 1024
F32 = jnp.float32
BF16 = jnp.bfloat16
HINT = pl.CostEstimate(flops=1000, bytes_accessed=1000, transcendentals=0)


def params(mib=58):
    return pltpu.CompilerParams(vmem_limit_bytes=mib * MIB)


def parts(x):
    high = x.astype(BF16)
    low = (x - high.astype(F32)).astype(BF16)
    return high, low


def gram_terms(x):
    high, low = parts(x)
    return lax.dot_general(
        high,
        jnp.concatenate([high, low], axis=1),
        (((0,), (0,)), ((), ())),
        preferred_element_type=F32,
    )


def gram_of_terms(terms):
    width = terms.shape[0]
    cross = terms[:, width:]
    return terms[:, :width] + cross + cross.T


def swapped(x, axis):
    return pltpu.roll(x, x.shape[axis] // 2, axis)


def times(x, weights):
    width = x.shape[1]
    both = jnp.dot(
        jnp.concatenate(parts(x), axis=1), weights, preferred_element_type=F32
    )
    return both[:, :width] + both[:, width:]


def weights_of(v):
    both = jnp.concatenate(parts(v), axis=1)
    return jnp.concatenate([both, both], axis=0)


def left_lanes(shape):
    return lax.broadcasted_iota(jnp.int32, shape, 1) < shape[1] // 2


def gram_kernel(x_ref, gram_ref, terms_ref):
    step = pl.program_id(0)

    @pl.when(step == 0)
    def _():
        terms_ref[...] = jnp.zeros_like(terms_ref)

    terms_ref[...] += gram_terms(x_ref[...])

    @pl.when(step == pl.num_programs(0) - 1)
    def _():
        gram_ref[...] = gram_of_terms(terms_ref[...])


def local_gram(x, block):
    rows, width = x.shape
    return pl.pallas_call(
        gram_kernel,
        grid=(rows // block,),
        in_specs=[pl.BlockSpec((block, width), lambda i: (i, 0))],
        out_specs=pl.BlockSpec((width, width), lambda i: (0, 0)),
        out_shape=jax.ShapeDtypeStruct((width, width), F32),
        scratch_shapes=[pltpu.VMEM((width, 2 * width), F32)],
        cost_estimate=HINT,
        compiler_params=params(),
    )(x)


def rotation_kernel(which, flags_ref, offsets_ref, one_ref, two_ref, a_ref, b_ref):
    gram = one_ref[...] + two_ref[...]
    width = gram.shape[0]
    half = width // 2
    row = lax.broadcasted_iota(jnp.int32, (width, width), 0)
    lane = lax.broadcasted_iota(jnp.int32, (width, width), 1)
    eye = row == lane
    is_first = lax.broadcasted_iota(jnp.int32, (1, width), 1) < half
    vectors = jnp.where(eye, 1.0, 0.0).astype(F32)
    dot = functools.partial(
        jnp.dot, precision=lax.Precision.HIGHEST, preferred_element_type=F32
    )
    for turn in range(ROUNDS):
        offset = offsets_ref[which, turn]
        above = lane + offset
        above = half + jnp.where(above >= half, above - half, above)
        below = lane - half - offset
        below = jnp.where(below < 0, below + half, below)
        pair = row == jnp.where(lane < half, above, below)
        own = jnp.sum(jnp.where(eye, gram, 0.0), axis=0, keepdims=True)
        own_col = jnp.sum(jnp.where(eye, gram, 0.0), axis=1, keepdims=True)
        other = jnp.sum(jnp.where(pair, own_col, 0.0), axis=0, keepdims=True)
        cross = jnp.sum(jnp.where(pair, gram, 0.0), axis=0, keepdims=True)
        spread = jnp.where(is_first, other - own, own - other)
        sign = jnp.where(spread >= 0.0, 1.0, -1.0)
        tangent = (
            sign
            * 2.0
            * cross
            / (jnp.abs(spread) + jnp.sqrt(spread * spread + 4.0 * cross * cross))
        )
        cosine = 1.0 / jnp.sqrt(1.0 + tangent * tangent)
        sine = tangent * cosine
        signed = jnp.where(is_first, -sine, sine)
        on_diagonal = jnp.where(eye, cosine, 0.0)
        off_diagonal = jnp.where(pair, signed, 0.0)
        turned = on_diagonal + off_diagonal
        vectors = dot(vectors, turned)
        if turn < ROUNDS - 1:
            gram = dot(on_diagonal - off_diagonal, dot(gram, turned))
    if which == 0:
        vectors = jnp.where(flags_ref[0] == 1, swapped(vectors, 1), vectors)
        other_vectors = swapped(vectors, 1)
    else:
        other_vectors = swapped(vectors, 0)
    a_ref[...] = weights_of(vectors)
    b_ref[...] = weights_of(other_vectors)


def rotations(which, flags, offsets, one, two):
    width = one.shape[0]
    smem = pl.BlockSpec(memory_space=pltpu.SMEM)
    vmem = pl.BlockSpec(memory_space=pltpu.VMEM)
    return pl.pallas_call(
        functools.partial(rotation_kernel, which),
        in_specs=[smem, smem, vmem, vmem],
        out_specs=[vmem, vmem],
        out_shape=[jax.ShapeDtypeStruct((2 * width, 2 * width), BF16)] * 2,
        cost_estimate=HINT,
        compiler_params=params(8),
    )(flags, offsets, one, two)


def run_spec(low, count, block, width):
    return pl.BlockSpec(
        (block, width), lambda i, f: (jnp.clip(i - low, 0, count - 1), 0)
    )


def first_product_kernel(runs, skip, flags_ref, x_ref, a_ref, b_ref, _, *out_refs):
    ya = times(x_ref[0], a_ref[...])
    yb = times(x_ref[1], b_ref[...])
    left = left_lanes(ya.shape)
    up = jnp.where(left, ya, yb)
    down = jnp.where(left, yb, ya)
    step = pl.program_id(0)
    for which, (low, count) in enumerate(runs):

        @pl.when((step >= low) & (step < low + count))
        def _():
            out_refs[2 * which][...] = up
            out_refs[2 * which + 1][...] = down

    if skip:
        out_refs[2 * len(runs)][...] = jnp.where(flags_ref[2] == 1, down, up)


def first_product(flags, x, a, b, earlier, start, block, runs, skip):
    width = x.shape[2]
    steps = sum(count for _, count in runs)
    first = start // block
    whole = pl.BlockSpec(a.shape, lambda i, f: (0, 0))
    out_specs, out_shape = [], []
    for low, count in [run for run in runs for _ in range(2)] + [(0, steps)] * skip:
        out_specs.append(run_spec(low, count, block, width))
        out_shape.append(jax.ShapeDtypeStruct((count * block, width), F32))
    return pl.pallas_call(
        functools.partial(first_product_kernel, runs, skip),
        grid_spec=pltpu.PrefetchScalarGridSpec(
            num_scalar_prefetch=1,
            grid=(steps,),
            in_specs=[
                pl.BlockSpec((2, block, width), lambda i, f: (0, i + first, 0)),
                whole,
                whole,
                pl.BlockSpec(memory_space=pl.ANY),
            ],
            out_specs=out_specs,
        ),
        out_shape=out_shape,
        cost_estimate=HINT,
        compiler_params=params(),
    )(flags, x, a, b, earlier)


def packed_gram_kernel(halves, flags_ref, *refs):
    *in_refs, gram_ref, a_ref, b_ref = refs
    step = pl.program_id(0)

    @pl.when(step == 0)
    def _():
        a_ref[...] = jnp.zeros_like(a_ref)
        b_ref[...] = jnp.zeros_like(b_ref)

    def add(first, second):
        left = left_lanes(first.shape)
        a_ref[...] += gram_terms(jnp.where(left, first, second))
        b_ref[...] += gram_terms(jnp.where(left, second, first))

    halves(step, flags_ref, add, *in_refs)

    @pl.when(step == pl.num_programs(0) - 1)
    def _():
        other = gram_of_terms(b_ref[...])
        gram_ref[...] = gram_of_terms(a_ref[...]) + swapped(swapped(other, 0), 1)


def neighbour_halves(early, step, flags_ref, add, got_ref, *own_refs):
    def with_own(u_ref, w_ref):
        own = jnp.where(flags_ref[2] == 1, u_ref[...], w_ref[...])
        at_end = flags_ref[0] + flags_ref[1]
        own = jnp.where(at_end == 1, swapped(own, 1), own)
        got = got_ref[...]
        own_first = flags_ref[3] == 1
        add(jnp.where(own_first, own, got), jnp.where(own_first, got, own))

    @pl.when(step < early)
    def _():
        with_own(*own_refs[:2])

    @pl.when(step >= early)
    def _():
        with_own(*own_refs[2:])


def arrived_halves(step, flags_ref, add, up_ref, down_ref, u_ref, w_ref):
    bottom = flags_ref[0] == 1
    top = flags_ref[1] == 1

    @pl.when(jnp.logical_not(jnp.logical_or(bottom, top)))
    def _():
        add(up_ref[...], down_ref[...])

    @pl.when(bottom)
    def _():
        add(swapped(w_ref[...], 1), down_ref[...])

    @pl.when(top)
    def _():
        add(up_ref[...], swapped(u_ref[...], 1))


def skipped_halves(step, flags_ref, add, up_ref, down_ref, u_ref, w_ref, got_ref):
    bottom = flags_ref[0] == 1
    top = flags_ref[1] == 1

    @pl.when(jnp.logical_not(jnp.logical_or(bottom, top)))
    def _():
        add(up_ref[...], down_ref[...])

    @pl.when(bottom)
    def _():
        add(swapped(w_ref[...], 1), got_ref[...])

    @pl.when(top)
    def _():
        add(got_ref[...], swapped(u_ref[...], 1))


def gram_call(halves, flags, operands, specs, steps):
    width = operands[0].shape[1]
    return pl.pallas_call(
        functools.partial(packed_gram_kernel, halves),
        grid_spec=pltpu.PrefetchScalarGridSpec(
            num_scalar_prefetch=1,
            grid=(steps,),
            in_specs=specs,
            out_specs=pl.BlockSpec((width, width), lambda i, f: (0, 0)),
            scratch_shapes=[pltpu.VMEM((width, 2 * width), F32)] * 2,
        ),
        out_shape=jax.ShapeDtypeStruct((width, width), F32),
        cost_estimate=HINT,
        compiler_params=params(),
    )(flags, *operands)


def neighbour_gram(flags, got, u2, w2, u3, w3, block):
    rows, width = got.shape
    early = u2.shape[0] // block
    late = u3.shape[0] // block
    one = run_spec(0, early, block, width)
    two = run_spec(early, late, block, width)
    every = run_spec(0, early + late, block, width)
    return gram_call(
        functools.partial(neighbour_halves, early),
        flags,
        [got, u2, w2, u3, w3],
        [every, one, one, two, two],
        early + late,
    )


def kept_spec(block, width):
    return pl.BlockSpec((block, width), lambda i, f: (i * (f[0] + f[1]), 0))


def arrived_gram(flags, up, down, u, w, block):
    rows, width = up.shape
    steps = rows // block
    every = run_spec(0, steps, block, width)
    kept = kept_spec(block, width)
    return gram_call(
        arrived_halves, flags, [up, down, u, w], [every, every, kept, kept], steps
    )


def second_product_kernel(halves, count, flags_ref, a_ref, b_ref, *refs):
    out_ref = refs[-1]

    def finish(first, second):
        left = left_lanes(first.shape)
        out_ref[0] = times(jnp.where(left, first, second), a_ref[...])
        out_ref[1] = times(jnp.where(left, second, first), b_ref[...])

    halves(pl.program_id(0), flags_ref, finish, *refs[:count])


def second_product(flags, a, b, operands, got, got_start, out, start, total, block):
    rows, width = operands[0].shape
    first = start // block
    got_first = got_start // block
    every = run_spec(0, rows // block, block, width)
    kept = kept_spec(block, width)
    whole = pl.BlockSpec(a.shape, lambda i, f: (0, 0))
    in_specs = [whole, whole, every, every, kept, kept]
    operands = list(operands)
    halves = arrived_halves
    if got is not None:
        halves = skipped_halves
        operands.append(got)
        in_specs.append(
            pl.BlockSpec(
                (block, width), lambda i, f: ((i + got_first) * (f[0] + f[1]), 0)
            )
        )
    count = len(operands)
    aliases = {}
    if out is not None:
        aliases = {3 + count: 0}
        operands.append(out)
        in_specs.append(pl.BlockSpec(memory_space=pl.ANY))
    return pl.pallas_call(
        functools.partial(second_product_kernel, halves, count),
        grid_spec=pltpu.PrefetchScalarGridSpec(
            num_scalar_prefetch=1,
            grid=(rows // block,),
            in_specs=in_specs,
            out_specs=pl.BlockSpec((2, block, width), lambda i, f: (0, i + first, 0)),
        ),
        out_shape=jax.ShapeDtypeStruct((2, total, width), F32),
        input_output_aliases=aliases,
        cost_estimate=HINT,
        compiler_params=params(),
    )(flags, a, b, *operands)


def row_partner(x, bit):
    size = lax.axis_size("rows")
    return lax.ppermute(x, "rows", [(i, i ^ bit) for i in range(size)])


def everywhere(x, target):
    rows, places = lax.axis_size("rows"), lax.axis_size("loop")
    pairs = []
    for row in range(rows):
        for place in range(places):
            where = target(row, place)
            pairs.append((row * places + place, where[0] * places + where[1]))
    return lax.ppermute(x, ("rows", "loop"), pairs)


def home(x, last):
    def onward(row, place):
        if place == 1:
            return row ^ 2, 0
        if place == last - 1:
            return row ^ 2, last
        return row, place - 2 if place % 2 else place + 2

    x = everywhere(x, lambda row, place: (row ^ 2, place ^ 1))
    return everywhere(x, onward)


def far_partner(x, count):
    ring = min(4, count // 2)

    def across(place):
        pair, odd = divmod(place, 2)
        group, at = divmod(pair, ring)
        at = (at - 1) % ring if odd else (at + 1) % ring
        return 2 * (group * ring + at) + 1 - odd

    x = everywhere(x, lambda row, place: (row, across(place)))
    return everywhere(x, lambda row, place: (row ^ 2, across(place)))


def held_kernel(*refs):
    pass


def held(arrays, earlier):
    anywhere = pl.BlockSpec(memory_space=pl.ANY)
    return pl.pallas_call(
        held_kernel,
        in_specs=[anywhere] * (len(arrays) + 1),
        out_specs=[anywhere] * len(arrays),
        out_shape=[jax.ShapeDtypeStruct(x.shape, x.dtype) for x in arrays],
        input_output_aliases={k: k for k in range(len(arrays))},
        cost_estimate=HINT,
        compiler_params=params(),
    )(*arrays, earlier)


def body(x, offsets):
    rows, width = x.shape
    half_rows = rows // 2
    large, small = half_rows // 6, half_rows // 12
    late, final = 8 * small, 11 * small
    place = lax.axis_index("loop")
    count = lax.axis_size("loop")
    last = count - 1
    odd = place % 2
    flags = jnp.stack(
        [
            (place == 0).astype(jnp.int32),
            (place == last).astype(jnp.int32),
            odd.astype(jnp.int32),
            ((place == 0) | ((odd == 1) & (place != last))).astype(jnp.int32),
        ]
    )
    halves = x.reshape(2, half_rows, width)

    ups = [(i, i + 1) for i in range(last)]
    downs = [(i, i - 1) for i in range(1, count)]
    skips = (
        [(i, i + 2) for i in range(0, last - 1, 2)]
        + [(i, i - 2) for i in range(3, count, 2)]
    )
    by_down, by_up = (25, 6) if count == 32 else (1, last - 1)

    gram = local_gram(x, rows // 3)
    gram = gram + row_partner(gram, 1)
    a, b = rotations(0, flags, offsets, gram, row_partner(gram, 2))

    u0, w0 = first_product(flags, halves, a, b, halves, 0, large, [(0, 4)], False)
    up0 = lax.ppermute(u0, "loop", ups)
    down0 = lax.ppermute(w0, "loop", downs)
    u1, w1, u2, w2, sent = first_product(
        flags, halves, a, b, u0, late, small, [(0, 3), (3, 1)], True
    )
    got = lax.ppermute(sent, "loop", skips)
    ends = lax.ppermute(sent, "loop", [(1, by_down), (last - 1, by_up)])
    (ends,) = held([ends], got)
    ends = lax.ppermute(ends, "loop", [(by_down, 0), (by_up, last)])
    got = jnp.where((place == 0) | (place == last), ends, got)

    gram = neighbour_gram(flags, got, u1, w1, u2, w2, small)
    u1, w1 = held([u1, w1], gram)
    up1 = lax.ppermute(u1, "loop", ups[:-1])
    down1 = lax.ppermute(w1, "loop", downs[1:])
    (gram,) = held([gram], up0)
    (gram,) = held([gram], down0)
    gram = home(gram, last)
    gram = gram + arrived_gram(flags, up0, down0, u0, w0, large)
    u2, w2 = held([u2, w2], gram)
    up2 = lax.ppermute(u2, "loop", ups[:-1])
    down2 = lax.ppermute(w2, "loop", downs[1:])
    gram = gram + row_partner(gram, 1)
    a, b = rotations(1, flags, offsets, gram, far_partner(gram, count))

    out = None
    for arrays, got_start, low, size in (
        ((up0, down0, u0, w0), None, 0, large),
        ((up1, down1, u1, w1), 0, late, small),
        ((up2, down2, u2, w2), final - late, final, small),
    ):
        skipped = None if got_start is None else got
        out = second_product(
            flags, a, b, arrays, skipped, got_start or 0, out, low, half_rows, size
        )
    return out.reshape(rows, width)


def solution(mesh):
    placed = (P("rows", "loop"), P())
    return jax.shard_map(
        body,
        mesh=mesh,
        in_specs=placed,
        out_specs=P("rows", "loop"),
        check_vma=False,
    )
```

```python
import functools

import jax
import jax.numpy as jnp
from jax import lax
from jax.experimental import pallas as pl
from jax.experimental.pallas import tpu as pltpu
from jax.sharding import PartitionSpec as P

ROUNDS = 4
MIB = 1024 * 1024
F32 = jnp.float32
BF16 = jnp.bfloat16
HINT = pl.CostEstimate(flops=1000, bytes_accessed=1000, transcendentals=0)


def params(mib=58):
    return pltpu.CompilerParams(vmem_limit_bytes=mib * MIB)


def parts(x):
    high = x.astype(BF16)
    low = (x - high.astype(F32)).astype(BF16)
    return high, low


def gram_terms(x):
    high, low = parts(x)
    return lax.dot_general(
        high,
        jnp.concatenate([high, low], axis=1),
        (((0,), (0,)), ((), ())),
        preferred_element_type=F32,
    )


def gram_of_terms(terms):
    width = terms.shape[0]
    cross = terms[:, width:]
    return terms[:, :width] + cross + cross.T


def swapped(x, axis):
    return pltpu.roll(x, x.shape[axis] // 2, axis)


def times(x, weights):
    width = x.shape[1]
    both = jnp.dot(
        jnp.concatenate(parts(x), axis=1), weights, preferred_element_type=F32
    )
    return both[:, :width] + both[:, width:]


def weights_of(v):
    both = jnp.concatenate(parts(v), axis=1)
    return jnp.concatenate([both, both], axis=0)


def left_lanes(shape):
    return lax.broadcasted_iota(jnp.int32, shape, 1) < shape[1] // 2


def gram_kernel(x_ref, gram_ref, terms_ref):
    step = pl.program_id(0)

    @pl.when(step == 0)
    def _():
        terms_ref[...] = jnp.zeros_like(terms_ref)

    terms_ref[...] += gram_terms(x_ref[...])

    @pl.when(step == pl.num_programs(0) - 1)
    def _():
        gram_ref[...] = gram_of_terms(terms_ref[...])


def local_gram(x, block):
    rows, width = x.shape
    return pl.pallas_call(
        gram_kernel,
        grid=(rows // block,),
        in_specs=[pl.BlockSpec((block, width), lambda i: (i, 0))],
        out_specs=pl.BlockSpec((width, width), lambda i: (0, 0)),
        out_shape=jax.ShapeDtypeStruct((width, width), F32),
        scratch_shapes=[pltpu.VMEM((width, 2 * width), F32)],
        cost_estimate=HINT,
        compiler_params=params(),
    )(x)


def rotation_kernel(which, flags_ref, offsets_ref, one_ref, two_ref, a_ref, b_ref):
    gram = one_ref[...] + two_ref[...]
    width = gram.shape[0]
    half = width // 2
    row = lax.broadcasted_iota(jnp.int32, (width, width), 0)
    lane = lax.broadcasted_iota(jnp.int32, (width, width), 1)
    eye = row == lane
    is_first = lax.broadcasted_iota(jnp.int32, (1, width), 1) < half
    vectors = jnp.where(eye, 1.0, 0.0).astype(F32)
    dot = functools.partial(
        jnp.dot, precision=lax.Precision.HIGHEST, preferred_element_type=F32
    )
    for turn in range(ROUNDS):
        offset = offsets_ref[which, turn]
        above = lane + offset
        above = half + jnp.where(above >= half, above - half, above)
        below = lane - half - offset
        below = jnp.where(below < 0, below + half, below)
        pair = row == jnp.where(lane < half, above, below)
        own = jnp.sum(jnp.where(eye, gram, 0.0), axis=0, keepdims=True)
        own_col = jnp.sum(jnp.where(eye, gram, 0.0), axis=1, keepdims=True)
        other = jnp.sum(jnp.where(pair, own_col, 0.0), axis=0, keepdims=True)
        cross = jnp.sum(jnp.where(pair, gram, 0.0), axis=0, keepdims=True)
        spread = jnp.where(is_first, other - own, own - other)
        sign = jnp.where(spread >= 0.0, 1.0, -1.0)
        tangent = (
            sign
            * 2.0
            * cross
            / (jnp.abs(spread) + jnp.sqrt(spread * spread + 4.0 * cross * cross))
        )
        cosine = 1.0 / jnp.sqrt(1.0 + tangent * tangent)
        sine = tangent * cosine
        signed = jnp.where(is_first, -sine, sine)
        on_diagonal = jnp.where(eye, cosine, 0.0)
        off_diagonal = jnp.where(pair, signed, 0.0)
        turned = on_diagonal + off_diagonal
        vectors = dot(vectors, turned)
        if turn < ROUNDS - 1:
            gram = dot(on_diagonal - off_diagonal, dot(gram, turned))
    if which == 0:
        vectors = jnp.where(flags_ref[0] == 1, swapped(vectors, 1), vectors)
        other_vectors = swapped(vectors, 1)
    else:
        other_vectors = swapped(vectors, 0)
    a_ref[...] = weights_of(vectors)
    b_ref[...] = weights_of(other_vectors)


def rotations(which, flags, offsets, one, two):
    width = one.shape[0]
    smem = pl.BlockSpec(memory_space=pltpu.SMEM)
    vmem = pl.BlockSpec(memory_space=pltpu.VMEM)
    return pl.pallas_call(
        functools.partial(rotation_kernel, which),
        in_specs=[smem, smem, vmem, vmem],
        out_specs=[vmem, vmem],
        out_shape=[jax.ShapeDtypeStruct((2 * width, 2 * width), BF16)] * 2,
        cost_estimate=HINT,
        compiler_params=params(8),
    )(flags, offsets, one, two)


def run_spec(low, count, block, width):
    return pl.BlockSpec(
        (block, width), lambda i, f: (jnp.clip(i - low, 0, count - 1), 0)
    )


def first_product_kernel(runs, skip, flags_ref, x_ref, a_ref, b_ref, _, *out_refs):
    ya = times(x_ref[0], a_ref[...])
    yb = times(x_ref[1], b_ref[...])
    left = left_lanes(ya.shape)
    up = jnp.where(left, ya, yb)
    down = jnp.where(left, yb, ya)
    step = pl.program_id(0)
    for which, (low, count) in enumerate(runs):

        @pl.when((step >= low) & (step < low + count))
        def _():
            out_refs[2 * which][...] = up
            out_refs[2 * which + 1][...] = down

    if skip:
        out_refs[2 * len(runs)][...] = jnp.where(flags_ref[2] == 1, down, up)


def first_product(flags, x, a, b, earlier, start, block, runs, skip):
    width = x.shape[2]
    steps = sum(count for _, count in runs)
    first = start // block
    whole = pl.BlockSpec(a.shape, lambda i, f: (0, 0))
    out_specs, out_shape = [], []
    for low, count in [run for run in runs for _ in range(2)] + [(0, steps)] * skip:
        out_specs.append(run_spec(low, count, block, width))
        out_shape.append(jax.ShapeDtypeStruct((count * block, width), F32))
    return pl.pallas_call(
        functools.partial(first_product_kernel, runs, skip),
        grid_spec=pltpu.PrefetchScalarGridSpec(
            num_scalar_prefetch=1,
            grid=(steps,),
            in_specs=[
                pl.BlockSpec((2, block, width), lambda i, f: (0, i + first, 0)),
                whole,
                whole,
                pl.BlockSpec(memory_space=pl.ANY),
            ],
            out_specs=out_specs,
        ),
        out_shape=out_shape,
        cost_estimate=HINT,
        compiler_params=params(),
    )(flags, x, a, b, earlier)


def packed_gram_kernel(halves, flags_ref, *refs):
    *in_refs, gram_ref, a_ref, b_ref = refs
    step = pl.program_id(0)

    @pl.when(step == 0)
    def _():
        a_ref[...] = jnp.zeros_like(a_ref)
        b_ref[...] = jnp.zeros_like(b_ref)

    def add(first, second):
        left = left_lanes(first.shape)
        a_ref[...] += gram_terms(jnp.where(left, first, second))
        b_ref[...] += gram_terms(jnp.where(left, second, first))

    halves(step, flags_ref, add, *in_refs)

    @pl.when(step == pl.num_programs(0) - 1)
    def _():
        other = gram_of_terms(b_ref[...])
        gram_ref[...] = gram_of_terms(a_ref[...]) + swapped(swapped(other, 0), 1)


def neighbour_halves(step, flags_ref, add, got_ref, u_ref, w_ref):
    own = jnp.where(flags_ref[2] == 1, u_ref[...], w_ref[...])
    at_end = flags_ref[0] + flags_ref[1]
    own = jnp.where(at_end == 1, swapped(own, 1), own)
    got = got_ref[...]
    own_first = flags_ref[3] == 1
    add(jnp.where(own_first, own, got), jnp.where(own_first, got, own))


def arrived_halves(step, flags_ref, add, up_ref, down_ref, u_ref, w_ref):
    bottom = flags_ref[0] == 1
    top = flags_ref[1] == 1

    @pl.when(jnp.logical_not(jnp.logical_or(bottom, top)))
    def _():
        add(up_ref[...], down_ref[...])

    @pl.when(bottom)
    def _():
        add(swapped(w_ref[...], 1), down_ref[...])

    @pl.when(top)
    def _():
        add(up_ref[...], swapped(u_ref[...], 1))


def skipped_halves(step, flags_ref, add, up_ref, down_ref, u_ref, w_ref, got_ref):
    bottom = flags_ref[0] == 1
    top = flags_ref[1] == 1

    @pl.when(jnp.logical_not(jnp.logical_or(bottom, top)))
    def _():
        add(up_ref[...], down_ref[...])

    @pl.when(bottom)
    def _():
        add(swapped(w_ref[...], 1), got_ref[...])

    @pl.when(top)
    def _():
        add(got_ref[...], swapped(u_ref[...], 1))


def gram_call(halves, flags, operands, specs, steps):
    width = operands[0].shape[1]
    return pl.pallas_call(
        functools.partial(packed_gram_kernel, halves),
        grid_spec=pltpu.PrefetchScalarGridSpec(
            num_scalar_prefetch=1,
            grid=(steps,),
            in_specs=specs,
            out_specs=pl.BlockSpec((width, width), lambda i, f: (0, 0)),
            scratch_shapes=[pltpu.VMEM((width, 2 * width), F32)] * 2,
        ),
        out_shape=jax.ShapeDtypeStruct((width, width), F32),
        cost_estimate=HINT,
        compiler_params=params(),
    )(flags, *operands)


def neighbour_gram(flags, got, u, w, block):
    rows, width = got.shape
    steps = rows // block
    every = run_spec(0, steps, block, width)
    return gram_call(neighbour_halves, flags, [got, u, w], [every] * 3, steps)


def kept_spec(block, width):
    return pl.BlockSpec((block, width), lambda i, f: (i * (f[0] + f[1]), 0))


def arrived_gram(flags, up, down, u, w, block):
    rows, width = up.shape
    steps = rows // block
    every = run_spec(0, steps, block, width)
    kept = kept_spec(block, width)
    return gram_call(
        arrived_halves, flags, [up, down, u, w], [every, every, kept, kept], steps
    )


def second_product_kernel(halves, count, flags_ref, a_ref, b_ref, *refs):
    out_ref = refs[-1]

    def finish(first, second):
        left = left_lanes(first.shape)
        out_ref[0] = times(jnp.where(left, first, second), a_ref[...])
        out_ref[1] = times(jnp.where(left, second, first), b_ref[...])

    halves(pl.program_id(0), flags_ref, finish, *refs[:count])


def second_product(flags, a, b, operands, got, got_start, out, start, total, block):
    rows, width = operands[0].shape
    first = start // block
    got_first = got_start // block
    every = run_spec(0, rows // block, block, width)
    kept = kept_spec(block, width)
    whole = pl.BlockSpec(a.shape, lambda i, f: (0, 0))
    in_specs = [whole, whole, every, every, kept, kept]
    operands = list(operands)
    halves = arrived_halves
    if got is not None:
        halves = skipped_halves
        operands.append(got)
        in_specs.append(
            pl.BlockSpec(
                (block, width), lambda i, f: ((i + got_first) * (f[0] + f[1]), 0)
            )
        )
    count = len(operands)
    aliases = {}
    if out is not None:
        aliases = {3 + count: 0}
        operands.append(out)
        in_specs.append(pl.BlockSpec(memory_space=pl.ANY))
    return pl.pallas_call(
        functools.partial(second_product_kernel, halves, count),
        grid_spec=pltpu.PrefetchScalarGridSpec(
            num_scalar_prefetch=1,
            grid=(rows // block,),
            in_specs=in_specs,
            out_specs=pl.BlockSpec((2, block, width), lambda i, f: (0, i + first, 0)),
        ),
        out_shape=jax.ShapeDtypeStruct((2, total, width), F32),
        input_output_aliases=aliases,
        cost_estimate=HINT,
        compiler_params=params(),
    )(flags, a, b, *operands)


def row_partner(x, bit):
    size = lax.axis_size("rows")
    return lax.ppermute(x, "rows", [(i, i ^ bit) for i in range(size)])


def everywhere(x, target):
    rows, places = lax.axis_size("rows"), lax.axis_size("loop")
    pairs = []
    for row in range(rows):
        for place in range(places):
            where = target(row, place)
            pairs.append((row * places + place, where[0] * places + where[1]))
    return lax.ppermute(x, ("rows", "loop"), pairs)


def home(x, last):
    def onward(row, place):
        if place == 1:
            return row ^ 2, 0
        if place == last - 1:
            return row ^ 2, last
        return row, place - 2 if place % 2 else place + 2

    x = everywhere(x, lambda row, place: (row ^ 2, place ^ 1))
    return everywhere(x, onward)


def far_partner(x, count):
    ring = min(4, count // 2)

    def across(place):
        pair, odd = divmod(place, 2)
        group, at = divmod(pair, ring)
        at = (at - 1) % ring if odd else (at + 1) % ring
        return 2 * (group * ring + at) + 1 - odd

    x = everywhere(x, lambda row, place: (row, across(place)))
    return everywhere(x, lambda row, place: (row ^ 2, across(place)))


def held_kernel(*refs):
    pass


def held(arrays, earlier):
    anywhere = pl.BlockSpec(memory_space=pl.ANY)
    return pl.pallas_call(
        held_kernel,
        in_specs=[anywhere] * (len(arrays) + 1),
        out_specs=[anywhere] * len(arrays),
        out_shape=[jax.ShapeDtypeStruct(x.shape, x.dtype) for x in arrays],
        input_output_aliases={k: k for k in range(len(arrays))},
        cost_estimate=HINT,
        compiler_params=params(),
    )(*arrays, earlier)


def body(x, offsets):
    rows, width = x.shape
    half_rows = rows // 2
    block = half_rows // 8
    late = 5 * block
    place = lax.axis_index("loop")
    count = lax.axis_size("loop")
    last = count - 1
    odd = place % 2
    flags = jnp.stack(
        [
            (place == 0).astype(jnp.int32),
            (place == last).astype(jnp.int32),
            odd.astype(jnp.int32),
            ((place == 0) | ((odd == 1) & (place != last))).astype(jnp.int32),
        ]
    )
    halves = x.reshape(2, half_rows, width)

    ups = [(i, i + 1) for i in range(last)]
    downs = [(i, i - 1) for i in range(1, count)]
    skips = (
        [(i, i + 2) for i in range(0, last - 1, 2)]
        + [(i, i - 2) for i in range(3, count, 2)]
    )
    by_down, by_up = (25, 6) if count == 32 else (1, last - 1)

    gram = local_gram(x, rows // 3)
    gram = gram + row_partner(gram, 1)
    a, b = rotations(0, flags, offsets, gram, row_partner(gram, 2))

    u0, w0 = first_product(flags, halves, a, b, halves, 0, block, [(0, 5)], False)
    up0 = lax.ppermute(u0, "loop", ups)
    down0 = lax.ppermute(w0, "loop", downs)
    u1, w1, sent = first_product(flags, halves, a, b, u0, late, block, [(0, 3)], True)
    got = lax.ppermute(sent, "loop", skips)
    ends = lax.ppermute(sent, "loop", [(1, by_down), (last - 1, by_up)])
    (ends,) = held([ends], got)
    ends = lax.ppermute(ends, "loop", [(by_down, 0), (by_up, last)])
    u1, w1 = held([u1, w1], got)
    up1 = lax.ppermute(u1, "loop", ups[:-1])
    down1 = lax.ppermute(w1, "loop", downs[1:])
    got = jnp.where((place == 0) | (place == last), ends, got)

    gram = neighbour_gram(flags, got, u1, w1, block)
    (gram,) = held([gram], up0)
    (gram,) = held([gram], down0)
    gram = home(gram, last)
    gram = gram + arrived_gram(flags, up0, down0, u0, w0, block)
    gram = gram + row_partner(gram, 1)
    a, b = rotations(1, flags, offsets, gram, far_partner(gram, count))

    out = second_product(
        flags, a, b, (up0, down0, u0, w0), None, 0, None, 0, half_rows, block
    )
    out = second_product(
        flags, a, b, (up1, down1, u1, w1), got, 0, out, late, half_rows, block
    )
    return out.reshape(rows, width)


def solution(mesh):
    placed = (P("rows", "loop"), P())
    return jax.shard_map(
        body,
        mesh=mesh,
        in_specs=placed,
        out_specs=P("rows", "loop"),
        check_vma=False,
    )
```

```python
import functools

import jax
import jax.numpy as jnp
from jax import lax
from jax.experimental import pallas as pl
from jax.experimental.pallas import tpu as pltpu
from jax.sharding import PartitionSpec as P

ROUNDS = 4
MIB = 1024 * 1024
F32 = jnp.float32
BF16 = jnp.bfloat16
HINT = pl.CostEstimate(flops=1000, bytes_accessed=1000, transcendentals=0)


def params(mib=58):
    return pltpu.CompilerParams(vmem_limit_bytes=mib * MIB)


def parts(x):
    high = x.astype(BF16)
    low = (x - high.astype(F32)).astype(BF16)
    return high, low


def gram_terms(x):
    high, low = parts(x)
    return lax.dot_general(
        high,
        jnp.concatenate([high, low], axis=1),
        (((0,), (0,)), ((), ())),
        preferred_element_type=F32,
    )


def gram_of_terms(terms):
    width = terms.shape[0]
    cross = terms[:, width:]
    return terms[:, :width] + cross + cross.T


def swapped(x, axis):
    return pltpu.roll(x, x.shape[axis] // 2, axis)


def times(x, weights):
    width = x.shape[1]
    both = jnp.dot(
        jnp.concatenate(parts(x), axis=1), weights, preferred_element_type=F32
    )
    return both[:, :width] + both[:, width:]


def weights_of(v):
    both = jnp.concatenate(parts(v), axis=1)
    return jnp.concatenate([both, both], axis=0)


def left_lanes(shape):
    return lax.broadcasted_iota(jnp.int32, shape, 1) < shape[1] // 2


def gram_kernel(x_ref, gram_ref, terms_ref):
    step = pl.program_id(0)

    @pl.when(step == 0)
    def _():
        terms_ref[...] = jnp.zeros_like(terms_ref)

    terms_ref[...] += gram_terms(x_ref[...])

    @pl.when(step == pl.num_programs(0) - 1)
    def _():
        gram_ref[...] = gram_of_terms(terms_ref[...])


def local_gram(x, block):
    rows, width = x.shape
    return pl.pallas_call(
        gram_kernel,
        grid=(rows // block,),
        in_specs=[pl.BlockSpec((block, width), lambda i: (i, 0))],
        out_specs=pl.BlockSpec((width, width), lambda i: (0, 0)),
        out_shape=jax.ShapeDtypeStruct((width, width), F32),
        scratch_shapes=[pltpu.VMEM((width, 2 * width), F32)],
        cost_estimate=HINT,
        compiler_params=params(),
    )(x)


def rotation_kernel(which, flags_ref, offsets_ref, one_ref, two_ref, a_ref, b_ref):
    gram = one_ref[...] + two_ref[...]
    width = gram.shape[0]
    half = width // 2
    row = lax.broadcasted_iota(jnp.int32, (width, width), 0)
    lane = lax.broadcasted_iota(jnp.int32, (width, width), 1)
    eye = row == lane
    is_first = lax.broadcasted_iota(jnp.int32, (1, width), 1) < half
    vectors = jnp.where(eye, 1.0, 0.0).astype(F32)
    dot = functools.partial(
        jnp.dot, precision=lax.Precision.HIGHEST, preferred_element_type=F32
    )
    for turn in range(ROUNDS):
        offset = offsets_ref[which, turn]
        above = lane + offset
        above = half + jnp.where(above >= half, above - half, above)
        below = lane - half - offset
        below = jnp.where(below < 0, below + half, below)
        pair = row == jnp.where(lane < half, above, below)
        own = jnp.sum(jnp.where(eye, gram, 0.0), axis=0, keepdims=True)
        own_col = jnp.sum(jnp.where(eye, gram, 0.0), axis=1, keepdims=True)
        other = jnp.sum(jnp.where(pair, own_col, 0.0), axis=0, keepdims=True)
        cross = jnp.sum(jnp.where(pair, gram, 0.0), axis=0, keepdims=True)
        spread = jnp.where(is_first, other - own, own - other)
        sign = jnp.where(spread >= 0.0, 1.0, -1.0)
        tangent = (
            sign
            * 2.0
            * cross
            / (jnp.abs(spread) + jnp.sqrt(spread * spread + 4.0 * cross * cross))
        )
        cosine = 1.0 / jnp.sqrt(1.0 + tangent * tangent)
        sine = tangent * cosine
        signed = jnp.where(is_first, -sine, sine)
        on_diagonal = jnp.where(eye, cosine, 0.0)
        off_diagonal = jnp.where(pair, signed, 0.0)
        turned = on_diagonal + off_diagonal
        vectors = dot(vectors, turned)
        if turn < ROUNDS - 1:
            gram = dot(on_diagonal - off_diagonal, dot(gram, turned))
    if which == 0:
        vectors = jnp.where(flags_ref[0] == 1, swapped(vectors, 1), vectors)
        other_vectors = swapped(vectors, 1)
    else:
        other_vectors = swapped(vectors, 0)
    a_ref[...] = weights_of(vectors)
    b_ref[...] = weights_of(other_vectors)


def rotations(which, flags, offsets, one, two):
    width = one.shape[0]
    smem = pl.BlockSpec(memory_space=pltpu.SMEM)
    vmem = pl.BlockSpec(memory_space=pltpu.VMEM)
    return pl.pallas_call(
        functools.partial(rotation_kernel, which),
        in_specs=[smem, smem, vmem, vmem],
        out_specs=[vmem, vmem],
        out_shape=[jax.ShapeDtypeStruct((2 * width, 2 * width), BF16)] * 2,
        cost_estimate=HINT,
        compiler_params=params(8),
    )(flags, offsets, one, two)


def run_spec(low, count, block, width):
    return pl.BlockSpec(
        (block, width), lambda i, f: (jnp.clip(i - low, 0, count - 1), 0)
    )


def first_product_kernel(runs, flags_ref, x_ref, a_ref, b_ref, *out_refs):
    ya = times(x_ref[0], a_ref[...])
    yb = times(x_ref[1], b_ref[...])
    left = left_lanes(ya.shape)
    up = jnp.where(left, ya, yb)
    down = jnp.where(left, yb, ya)
    step = pl.program_id(0)
    for which, (low, count) in enumerate(runs):

        @pl.when((step >= low) & (step < low + count))
        def _():
            out_refs[2 * which][...] = up
            out_refs[2 * which + 1][...] = down

    @pl.when(step >= runs[-1][0])
    def _():
        out_refs[-1][...] = jnp.where(flags_ref[2] == 1, down, up)


def first_product(flags, x, a, b, block, runs):
    width = x.shape[2]
    steps = sum(count for _, count in runs)
    whole = pl.BlockSpec(a.shape, lambda i, f: (0, 0))
    out_specs, out_shape = [], []
    for low, count in [run for run in runs for _ in range(2)] + runs[-1:]:
        out_specs.append(run_spec(low, count, block, width))
        out_shape.append(jax.ShapeDtypeStruct((count * block, width), F32))
    return pl.pallas_call(
        functools.partial(first_product_kernel, runs),
        grid_spec=pltpu.PrefetchScalarGridSpec(
            num_scalar_prefetch=1,
            grid=(steps,),
            in_specs=[
                pl.BlockSpec((2, block, width), lambda i, f: (0, i, 0)),
                whole,
                whole,
            ],
            out_specs=out_specs,
        ),
        out_shape=out_shape,
        cost_estimate=HINT,
        compiler_params=params(48),
    )(flags, x, a, b)


def packed_gram_kernel(halves, flags_ref, *refs):
    *in_refs, gram_ref, a_ref, b_ref = refs
    step = pl.program_id(0)

    @pl.when(step == 0)
    def _():
        a_ref[...] = jnp.zeros_like(a_ref)
        b_ref[...] = jnp.zeros_like(b_ref)

    def add(first, second):
        left = left_lanes(first.shape)
        a_ref[...] += gram_terms(jnp.where(left, first, second))
        b_ref[...] += gram_terms(jnp.where(left, second, first))

    halves(step, flags_ref, add, *in_refs)

    @pl.when(step == pl.num_programs(0) - 1)
    def _():
        other = gram_of_terms(b_ref[...])
        gram_ref[...] = gram_of_terms(a_ref[...]) + swapped(swapped(other, 0), 1)


def neighbour_halves(step, flags_ref, add, got_ref, u_ref, w_ref):
    own = jnp.where(flags_ref[2] == 1, u_ref[...], w_ref[...])
    at_end = flags_ref[0] + flags_ref[1]
    own = jnp.where(at_end == 1, swapped(own, 1), own)
    got = got_ref[...]
    own_first = flags_ref[3] == 1
    add(jnp.where(own_first, own, got), jnp.where(own_first, got, own))


def arrived_halves(step, flags_ref, add, up_ref, down_ref, u_ref, w_ref):
    bottom = flags_ref[0] == 1
    top = flags_ref[1] == 1

    @pl.when(jnp.logical_not(jnp.logical_or(bottom, top)))
    def _():
        add(up_ref[...], down_ref[...])

    @pl.when(bottom)
    def _():
        add(swapped(w_ref[...], 1), down_ref[...])

    @pl.when(top)
    def _():
        add(up_ref[...], swapped(u_ref[...], 1))


def skipped_halves(step, flags_ref, add, up_ref, down_ref, u_ref, w_ref, got_ref):
    bottom = flags_ref[0] == 1
    top = flags_ref[1] == 1

    @pl.when(jnp.logical_not(jnp.logical_or(bottom, top)))
    def _():
        add(up_ref[...], down_ref[...])

    @pl.when(bottom)
    def _():
        add(swapped(w_ref[...], 1), got_ref[...])

    @pl.when(top)
    def _():
        add(got_ref[...], swapped(u_ref[...], 1))


def gram_call(halves, flags, operands, specs, steps):
    width = operands[0].shape[1]
    return pl.pallas_call(
        functools.partial(packed_gram_kernel, halves),
        grid_spec=pltpu.PrefetchScalarGridSpec(
            num_scalar_prefetch=1,
            grid=(steps,),
            in_specs=specs,
            out_specs=pl.BlockSpec((width, width), lambda i, f: (0, 0)),
            scratch_shapes=[pltpu.VMEM((width, 2 * width), F32)] * 2,
        ),
        out_shape=jax.ShapeDtypeStruct((width, width), F32),
        cost_estimate=HINT,
        compiler_params=params(),
    )(flags, *operands)


def neighbour_gram(flags, got, u, w, block):
    rows, width = got.shape
    steps = rows // block
    every = run_spec(0, steps, block, width)
    return gram_call(neighbour_halves, flags, [got, u, w], [every] * 3, steps)


def kept_spec(block, width):
    return pl.BlockSpec((block, width), lambda i, f: (i * (f[0] + f[1]), 0))


def arrived_gram(flags, up, down, u, w, block):
    rows, width = up.shape
    steps = rows // block
    every = run_spec(0, steps, block, width)
    kept = kept_spec(block, width)
    return gram_call(
        arrived_halves, flags, [up, down, u, w], [every, every, kept, kept], steps
    )


def second_product_kernel(halves, count, flags_ref, a_ref, b_ref, *refs):
    out_ref = refs[-1]

    def finish(first, second):
        left = left_lanes(first.shape)
        out_ref[0] = times(jnp.where(left, first, second), a_ref[...])
        out_ref[1] = times(jnp.where(left, second, first), b_ref[...])

    halves(pl.program_id(0), flags_ref, finish, *refs[:count])


def second_product(flags, a, b, operands, got, got_start, out, start, total, block):
    rows, width = operands[0].shape
    first = start // block
    got_first = got_start // block
    every = run_spec(0, rows // block, block, width)
    kept = kept_spec(block, width)
    whole = pl.BlockSpec(a.shape, lambda i, f: (0, 0))
    in_specs = [whole, whole, every, every, kept, kept]
    operands = list(operands)
    halves = arrived_halves
    if got is not None:
        halves = skipped_halves
        operands.append(got)
        in_specs.append(
            pl.BlockSpec(
                (block, width), lambda i, f: ((i + got_first) * (f[0] + f[1]), 0)
            )
        )
    count = len(operands)
    aliases = {}
    if out is not None:
        aliases = {3 + count: 0}
        operands.append(out)
        in_specs.append(pl.BlockSpec(memory_space=pl.ANY))
    return pl.pallas_call(
        functools.partial(second_product_kernel, halves, count),
        grid_spec=pltpu.PrefetchScalarGridSpec(
            num_scalar_prefetch=1,
            grid=(rows // block,),
            in_specs=in_specs,
            out_specs=pl.BlockSpec((2, block, width), lambda i, f: (0, i + first, 0)),
        ),
        out_shape=jax.ShapeDtypeStruct((2, total, width), F32),
        input_output_aliases=aliases,
        cost_estimate=HINT,
        compiler_params=params(48),
    )(flags, a, b, *operands)


def row_partner(x, bit):
    size = lax.axis_size("rows")
    return lax.ppermute(x, "rows", [(i, i ^ bit) for i in range(size)])


def everywhere(x, target):
    rows, places = lax.axis_size("rows"), lax.axis_size("loop")
    pairs = []
    for row in range(rows):
        for place in range(places):
            where = target(row, place)
            pairs.append((row * places + place, where[0] * places + where[1]))
    return lax.ppermute(x, ("rows", "loop"), pairs)


def home(x, last):
    def onward(row, place):
        if place == 1:
            return row ^ 2, 0
        if place == last - 1:
            return row ^ 2, last
        return row, place - 2 if place % 2 else place + 2

    x = everywhere(x, lambda row, place: (row ^ 2, place ^ 1))
    return everywhere(x, onward)


def far_partner(x, count):
    ring = min(4, count // 2)

    def across(place):
        pair, odd = divmod(place, 2)
        group, at = divmod(pair, ring)
        at = (at - 1) % ring if odd else (at + 1) % ring
        return 2 * (group * ring + at) + 1 - odd

    x = everywhere(x, lambda row, place: (row, across(place)))
    return everywhere(x, lambda row, place: (row ^ 2, across(place)))


def held_kernel(*refs):
    pass


def held(arrays, earlier):
    anywhere = pl.BlockSpec(memory_space=pl.ANY)
    return pl.pallas_call(
        held_kernel,
        in_specs=[anywhere] * (len(arrays) + 1),
        out_specs=[anywhere] * len(arrays),
        out_shape=[jax.ShapeDtypeStruct(x.shape, x.dtype) for x in arrays],
        input_output_aliases={k: k for k in range(len(arrays))},
        cost_estimate=HINT,
        compiler_params=params(),
    )(*arrays, earlier)


def body(x, offsets):
    rows, width = x.shape
    half_rows = rows // 2
    block = half_rows // 8
    late = 5 * block
    place = lax.axis_index("loop")
    count = lax.axis_size("loop")
    last = count - 1
    odd = place % 2
    flags = jnp.stack(
        [
            (place == 0).astype(jnp.int32),
            (place == last).astype(jnp.int32),
            odd.astype(jnp.int32),
            ((place == 0) | ((odd == 1) & (place != last))).astype(jnp.int32),
        ]
    )
    halves = x.reshape(2, half_rows, width)

    ups = [(i, i + 1) for i in range(last)]
    downs = [(i, i - 1) for i in range(1, count)]
    skips = (
        [(i, i + 2) for i in range(0, last - 1, 2)]
        + [(i, i - 2) for i in range(3, count, 2)]
    )
    by_down, by_up = (25, 6) if count == 32 else (1, last - 1)

    gram = local_gram(x, rows // 3)
    gram = gram + row_partner(gram, 1)
    a, b = rotations(0, flags, offsets, gram, row_partner(gram, 2))

    u0, w0, u1, w1, sent = first_product(
        flags, halves, a, b, block, [(0, 5), (5, 3)]
    )
    up0 = lax.ppermute(u0, "loop", ups)
    down0 = lax.ppermute(w0, "loop", downs)
    got = lax.ppermute(sent, "loop", skips)
    ends = lax.ppermute(sent, "loop", [(1, by_down), (last - 1, by_up)])
    (ends,) = held([ends], got)
    ends = lax.ppermute(ends, "loop", [(by_down, 0), (by_up, last)])
    u1, w1 = held([u1, w1], got)
    up1 = lax.ppermute(u1, "loop", ups[:-1])
    down1 = lax.ppermute(w1, "loop", downs[1:])
    got = jnp.where((place == 0) | (place == last), ends, got)

    gram = neighbour_gram(flags, got, u1, w1, block)
    (gram,) = held([gram], up0)
    (gram,) = held([gram], down0)
    gram = home(gram, last)
    gram = gram + arrived_gram(flags, up0, down0, u0, w0, block)
    gram = gram + row_partner(gram, 1)
    a, b = rotations(1, flags, offsets, gram, far_partner(gram, count))

    out = second_product(
        flags, a, b, (up0, down0, u0, w0), None, 0, None, 0, half_rows, block
    )
    out = second_product(
        flags, a, b, (up1, down1, u1, w1), got, 0, out, late, half_rows, block
    )
    return out.reshape(rows, width)


def solution(mesh):
    placed = (P("rows", "loop"), P())
    return jax.shard_map(
        body,
        mesh=mesh,
        in_specs=placed,
        out_specs=P("rows", "loop"),
        check_vma=False,
    )
```

```python
import functools

import jax
import jax.numpy as jnp
from jax import lax
from jax.experimental import pallas as pl
from jax.experimental.pallas import tpu as pltpu
from jax.sharding import PartitionSpec as P

ROUNDS = 4
MIB = 1024 * 1024
F32 = jnp.float32
BF16 = jnp.bfloat16
HINT = pl.CostEstimate(flops=1000, bytes_accessed=1000, transcendentals=0)


def params(mib=58):
    return pltpu.CompilerParams(vmem_limit_bytes=mib * MIB)


def parts(x):
    high = x.astype(BF16)
    low = (x - high.astype(F32)).astype(BF16)
    return high, low


def gram_terms(x):
    high, low = parts(x)
    return lax.dot_general(
        high,
        jnp.concatenate([high, low], axis=1),
        (((0,), (0,)), ((), ())),
        preferred_element_type=F32,
    )


def gram_of_terms(terms):
    width = terms.shape[0]
    cross = terms[:, width:]
    return terms[:, :width] + cross + cross.T


def swapped(x, axis):
    return pltpu.roll(x, x.shape[axis] // 2, axis)


def times(x, weights):
    width = x.shape[1]
    both = jnp.dot(
        jnp.concatenate(parts(x), axis=1), weights, preferred_element_type=F32
    )
    return both[:, :width] + both[:, width:]


def weights_of(v):
    both = jnp.concatenate(parts(v), axis=1)
    return jnp.concatenate([both, both], axis=0)


def left_lanes(shape):
    return lax.broadcasted_iota(jnp.int32, shape, 1) < shape[1] // 2


def gram_kernel(x_ref, gram_ref, terms_ref):
    step = pl.program_id(0)

    @pl.when(step == 0)
    def _():
        terms_ref[...] = jnp.zeros_like(terms_ref)

    terms_ref[...] += gram_terms(x_ref[...])

    @pl.when(step == pl.num_programs(0) - 1)
    def _():
        gram_ref[...] = gram_of_terms(terms_ref[...])


def local_gram(x, block):
    rows, width = x.shape
    return pl.pallas_call(
        gram_kernel,
        grid=(rows // block,),
        in_specs=[pl.BlockSpec((block, width), lambda i: (i, 0))],
        out_specs=pl.BlockSpec((width, width), lambda i: (0, 0)),
        out_shape=jax.ShapeDtypeStruct((width, width), F32),
        scratch_shapes=[pltpu.VMEM((width, 2 * width), F32)],
        cost_estimate=HINT,
        compiler_params=params(),
    )(x)


def rotation_kernel(which, flags_ref, offsets_ref, one_ref, two_ref, a_ref, b_ref):
    gram = one_ref[...] + two_ref[...]
    width = gram.shape[0]
    half = width // 2
    row = lax.broadcasted_iota(jnp.int32, (width, width), 0)
    lane = lax.broadcasted_iota(jnp.int32, (width, width), 1)
    eye = row == lane
    is_first = lax.broadcasted_iota(jnp.int32, (1, width), 1) < half
    vectors = jnp.where(eye, 1.0, 0.0).astype(F32)
    dot = functools.partial(
        jnp.dot, precision=lax.Precision.HIGHEST, preferred_element_type=F32
    )
    for turn in range(ROUNDS):
        offset = offsets_ref[which, turn]
        above = lane + offset
        above = half + jnp.where(above >= half, above - half, above)
        below = lane - half - offset
        below = jnp.where(below < 0, below + half, below)
        pair = row == jnp.where(lane < half, above, below)
        own = jnp.sum(jnp.where(eye, gram, 0.0), axis=0, keepdims=True)
        own_col = jnp.sum(jnp.where(eye, gram, 0.0), axis=1, keepdims=True)
        other = jnp.sum(jnp.where(pair, own_col, 0.0), axis=0, keepdims=True)
        cross = jnp.sum(jnp.where(pair, gram, 0.0), axis=0, keepdims=True)
        spread = jnp.where(is_first, other - own, own - other)
        sign = jnp.where(spread >= 0.0, 1.0, -1.0)
        tangent = (
            sign
            * 2.0
            * cross
            / (jnp.abs(spread) + jnp.sqrt(spread * spread + 4.0 * cross * cross))
        )
        cosine = 1.0 / jnp.sqrt(1.0 + tangent * tangent)
        sine = tangent * cosine
        signed = jnp.where(is_first, -sine, sine)
        on_diagonal = jnp.where(eye, cosine, 0.0)
        off_diagonal = jnp.where(pair, signed, 0.0)
        turned = on_diagonal + off_diagonal
        vectors = dot(vectors, turned)
        if turn < ROUNDS - 1:
            gram = dot(on_diagonal - off_diagonal, dot(gram, turned))
    if which == 0:
        vectors = jnp.where(flags_ref[0] == 1, swapped(vectors, 1), vectors)
        other_vectors = swapped(vectors, 1)
    else:
        other_vectors = swapped(vectors, 0)
    a_ref[...] = weights_of(vectors)
    b_ref[...] = weights_of(other_vectors)


def rotations(which, flags, offsets, one, two):
    width = one.shape[0]
    smem = pl.BlockSpec(memory_space=pltpu.SMEM)
    vmem = pl.BlockSpec(memory_space=pltpu.VMEM)
    return pl.pallas_call(
        functools.partial(rotation_kernel, which),
        in_specs=[smem, smem, vmem, vmem],
        out_specs=[vmem, vmem],
        out_shape=[jax.ShapeDtypeStruct((2 * width, 2 * width), BF16)] * 2,
        cost_estimate=HINT,
        compiler_params=params(8),
    )(flags, offsets, one, two)


def run_spec(low, count, block, width):
    return pl.BlockSpec(
        (block, width), lambda i, f: (jnp.clip(i - low, 0, count - 1), 0)
    )


def first_product_kernel(runs, flags_ref, x_ref, a_ref, b_ref, *out_refs):
    ya = times(x_ref[0], a_ref[...])
    yb = times(x_ref[1], b_ref[...])
    left = left_lanes(ya.shape)
    up = jnp.where(left, ya, yb)
    down = jnp.where(left, yb, ya)
    step = pl.program_id(0)
    for which, (low, count) in enumerate(runs):

        @pl.when((step >= low) & (step < low + count))
        def _():
            out_refs[2 * which][...] = up
            out_refs[2 * which + 1][...] = down

    @pl.when(step >= runs[-1][0])
    def _():
        out_refs[-1][...] = jnp.where(flags_ref[2] == 1, down, up)


def first_product(flags, x, a, b, block, runs):
    width = x.shape[2]
    steps = sum(count for _, count in runs)
    whole = pl.BlockSpec(a.shape, lambda i, f: (0, 0))
    out_specs, out_shape = [], []
    for low, count in [run for run in runs for _ in range(2)] + runs[-1:]:
        out_specs.append(run_spec(low, count, block, width))
        out_shape.append(jax.ShapeDtypeStruct((count * block, width), F32))
    return pl.pallas_call(
        functools.partial(first_product_kernel, runs),
        grid_spec=pltpu.PrefetchScalarGridSpec(
            num_scalar_prefetch=1,
            grid=(steps,),
            in_specs=[
                pl.BlockSpec((2, block, width), lambda i, f: (0, i, 0)),
                whole,
                whole,
            ],
            out_specs=out_specs,
        ),
        out_shape=out_shape,
        cost_estimate=HINT,
        compiler_params=params(52),
    )(flags, x, a, b)


def packed_gram_kernel(halves, flags_ref, *refs):
    *in_refs, gram_ref, a_ref, b_ref = refs
    step = pl.program_id(0)

    @pl.when(step == 0)
    def _():
        a_ref[...] = jnp.zeros_like(a_ref)
        b_ref[...] = jnp.zeros_like(b_ref)

    def add(first, second):
        left = left_lanes(first.shape)
        a_ref[...] += gram_terms(jnp.where(left, first, second))
        b_ref[...] += gram_terms(jnp.where(left, second, first))

    halves(step, flags_ref, add, *in_refs)

    @pl.when(step == pl.num_programs(0) - 1)
    def _():
        other = gram_of_terms(b_ref[...])
        gram_ref[...] = gram_of_terms(a_ref[...]) + swapped(swapped(other, 0), 1)


def neighbour_halves(step, flags_ref, add, got_ref, u_ref, w_ref):
    own = jnp.where(flags_ref[2] == 1, u_ref[...], w_ref[...])
    at_end = flags_ref[0] + flags_ref[1]
    own = jnp.where(at_end == 1, swapped(own, 1), own)
    got = got_ref[...]
    own_first = flags_ref[3] == 1
    add(jnp.where(own_first, own, got), jnp.where(own_first, got, own))


def arrived_halves(step, flags_ref, add, up_ref, down_ref, u_ref, w_ref):
    bottom = flags_ref[0] == 1
    top = flags_ref[1] == 1

    @pl.when(jnp.logical_not(jnp.logical_or(bottom, top)))
    def _():
        add(up_ref[...], down_ref[...])

    @pl.when(bottom)
    def _():
        add(swapped(w_ref[...], 1), down_ref[...])

    @pl.when(top)
    def _():
        add(up_ref[...], swapped(u_ref[...], 1))


def skipped_halves(step, flags_ref, add, up_ref, down_ref, u_ref, w_ref, got_ref):
    bottom = flags_ref[0] == 1
    top = flags_ref[1] == 1

    @pl.when(jnp.logical_not(jnp.logical_or(bottom, top)))
    def _():
        add(up_ref[...], down_ref[...])

    @pl.when(bottom)
    def _():
        add(swapped(w_ref[...], 1), got_ref[...])

    @pl.when(top)
    def _():
        add(got_ref[...], swapped(u_ref[...], 1))


def gram_call(halves, flags, operands, specs, steps):
    width = operands[0].shape[1]
    return pl.pallas_call(
        functools.partial(packed_gram_kernel, halves),
        grid_spec=pltpu.PrefetchScalarGridSpec(
            num_scalar_prefetch=1,
            grid=(steps,),
            in_specs=specs,
            out_specs=pl.BlockSpec((width, width), lambda i, f: (0, 0)),
            scratch_shapes=[pltpu.VMEM((width, 2 * width), F32)] * 2,
        ),
        out_shape=jax.ShapeDtypeStruct((width, width), F32),
        cost_estimate=HINT,
        compiler_params=params(),
    )(flags, *operands)


def neighbour_gram(flags, got, u, w, block):
    rows, width = got.shape
    steps = rows // block
    every = run_spec(0, steps, block, width)
    return gram_call(neighbour_halves, flags, [got, u, w], [every] * 3, steps)


def kept_spec(block, width):
    return pl.BlockSpec((block, width), lambda i, f: (i * (f[0] + f[1]), 0))


def arrived_gram(flags, up, down, u, w, block):
    rows, width = up.shape
    steps = rows // block
    every = run_spec(0, steps, block, width)
    kept = kept_spec(block, width)
    return gram_call(
        arrived_halves, flags, [up, down, u, w], [every, every, kept, kept], steps
    )


def second_product_kernel(halves, count, flags_ref, a_ref, b_ref, *refs):
    out_ref = refs[-1]

    def finish(first, second):
        left = left_lanes(first.shape)
        out_ref[0] = times(jnp.where(left, first, second), a_ref[...])
        out_ref[1] = times(jnp.where(left, second, first), b_ref[...])

    halves(pl.program_id(0), flags_ref, finish, *refs[:count])


def second_product(flags, a, b, operands, got, got_start, out, start, total, block):
    rows, width = operands[0].shape
    first = start // block
    got_first = got_start // block
    every = run_spec(0, rows // block, block, width)
    kept = kept_spec(block, width)
    whole = pl.BlockSpec(a.shape, lambda i, f: (0, 0))
    in_specs = [whole, whole, every, every, kept, kept]
    operands = list(operands)
    halves = arrived_halves
    if got is not None:
        halves = skipped_halves
        operands.append(got)
        in_specs.append(
            pl.BlockSpec(
                (block, width), lambda i, f: ((i + got_first) * (f[0] + f[1]), 0)
            )
        )
    count = len(operands)
    aliases = {}
    if out is not None:
        aliases = {3 + count: 0}
        operands.append(out)
        in_specs.append(pl.BlockSpec(memory_space=pl.ANY))
    return pl.pallas_call(
        functools.partial(second_product_kernel, halves, count),
        grid_spec=pltpu.PrefetchScalarGridSpec(
            num_scalar_prefetch=1,
            grid=(rows // block,),
            in_specs=in_specs,
            out_specs=pl.BlockSpec((2, block, width), lambda i, f: (0, i + first, 0)),
        ),
        out_shape=jax.ShapeDtypeStruct((2, total, width), F32),
        input_output_aliases=aliases,
        cost_estimate=HINT,
        compiler_params=params(52),
    )(flags, a, b, *operands)


def row_partner(x, bit):
    size = lax.axis_size("rows")
    return lax.ppermute(x, "rows", [(i, i ^ bit) for i in range(size)])


def everywhere(x, target):
    rows, places = lax.axis_size("rows"), lax.axis_size("loop")
    pairs = []
    for row in range(rows):
        for place in range(places):
            where = target(row, place)
            pairs.append((row * places + place, where[0] * places + where[1]))
    return lax.ppermute(x, ("rows", "loop"), pairs)


def home(x, last):
    def onward(row, place):
        if place == 1:
            return row ^ 2, 0
        if place == last - 1:
            return row ^ 2, last
        return row, place - 2 if place % 2 else place + 2

    x = everywhere(x, lambda row, place: (row ^ 2, place ^ 1))
    return everywhere(x, onward)


def far_partner(x, count):
    ring = min(4, count // 2)

    def across(place):
        pair, odd = divmod(place, 2)
        group, at = divmod(pair, ring)
        at = (at - 1) % ring if odd else (at + 1) % ring
        return 2 * (group * ring + at) + 1 - odd

    x = everywhere(x, lambda row, place: (row, across(place)))
    return everywhere(x, lambda row, place: (row ^ 2, across(place)))


def held_kernel(*refs):
    pass


def held(arrays, earlier):
    anywhere = pl.BlockSpec(memory_space=pl.ANY)
    return pl.pallas_call(
        held_kernel,
        in_specs=[anywhere] * (len(arrays) + 1),
        out_specs=[anywhere] * len(arrays),
        out_shape=[jax.ShapeDtypeStruct(x.shape, x.dtype) for x in arrays],
        input_output_aliases={k: k for k in range(len(arrays))},
        cost_estimate=HINT,
        compiler_params=params(),
    )(*arrays, earlier)


def body(x, offsets):
    rows, width = x.shape
    half_rows = rows // 2
    block = half_rows // 8
    late = 5 * block
    place = lax.axis_index("loop")
    count = lax.axis_size("loop")
    last = count - 1
    odd = place % 2
    flags = jnp.stack(
        [
            (place == 0).astype(jnp.int32),
            (place == last).astype(jnp.int32),
            odd.astype(jnp.int32),
            ((place == 0) | ((odd == 1) & (place != last))).astype(jnp.int32),
        ]
    )
    halves = x.reshape(2, half_rows, width)

    ups = [(i, i + 1) for i in range(last)]
    downs = [(i, i - 1) for i in range(1, count)]
    skips = (
        [(i, i + 2) for i in range(0, last - 1, 2)]
        + [(i, i - 2) for i in range(3, count, 2)]
    )
    by_down, by_up = (25, 6) if count == 32 else (1, last - 1)

    gram = local_gram(x, rows // 3)
    gram = gram + row_partner(gram, 1)
    a, b = rotations(0, flags, offsets, gram, row_partner(gram, 2))

    u0, w0, u1, w1, sent = first_product(
        flags, halves, a, b, block, [(0, 5), (5, 3)]
    )
    up0 = lax.ppermute(u0, "loop", ups)
    down0 = lax.ppermute(w0, "loop", downs)
    got = lax.ppermute(sent, "loop", skips)
    ends = lax.ppermute(sent, "loop", [(1, by_down), (last - 1, by_up)])
    (ends,) = held([ends], got)
    ends = lax.ppermute(ends, "loop", [(by_down, 0), (by_up, last)])
    u1, w1 = held([u1, w1], got)
    up1 = lax.ppermute(u1, "loop", ups[:-1])
    down1 = lax.ppermute(w1, "loop", downs[1:])
    got = jnp.where((place == 0) | (place == last), ends, got)

    gram = neighbour_gram(flags, got, u1, w1, block)
    (gram,) = held([gram], up0)
    (gram,) = held([gram], down0)
    gram = home(gram, last)
    gram = gram + arrived_gram(flags, up0, down0, u0, w0, block)
    gram = gram + row_partner(gram, 1)
    a, b = rotations(1, flags, offsets, gram, far_partner(gram, count))

    out = second_product(
        flags, a, b, (up0, down0, u0, w0), None, 0, None, 0, half_rows, block
    )
    out = second_product(
        flags, a, b, (up1, down1, u1, w1), got, 0, out, late, half_rows, block
    )
    return out.reshape(rows, width)


def solution(mesh):
    placed = (P("rows", "loop"), P())
    return jax.shard_map(
        body,
        mesh=mesh,
        in_specs=placed,
        out_specs=P("rows", "loop"),
        check_vma=False,
    )
```

```python
import functools

import jax
import jax.numpy as jnp
from jax import lax
from jax.experimental import pallas as pl
from jax.experimental.pallas import tpu as pltpu
from jax.sharding import PartitionSpec as P

ROUNDS = 4
MIB = 1024 * 1024
F32 = jnp.float32
BF16 = jnp.bfloat16
HINT = pl.CostEstimate(flops=1000, bytes_accessed=1000, transcendentals=0)


def params(mib=58):
    return pltpu.CompilerParams(vmem_limit_bytes=mib * MIB)


def parts(x):
    high = x.astype(BF16)
    low = (x - high.astype(F32)).astype(BF16)
    return high, low


def gram_terms(x):
    high, low = parts(x)
    return lax.dot_general(
        high,
        jnp.concatenate([high, low], axis=1),
        (((0,), (0,)), ((), ())),
        preferred_element_type=F32,
    )


def gram_of_terms(terms):
    width = terms.shape[0]
    cross = terms[:, width:]
    return terms[:, :width] + cross + cross.T


def swapped(x, axis):
    return pltpu.roll(x, x.shape[axis] // 2, axis)


def times(x, weights):
    width = x.shape[1]
    both = jnp.dot(
        jnp.concatenate(parts(x), axis=1), weights, preferred_element_type=F32
    )
    return both[:, :width] + both[:, width:]


def weights_of(v):
    both = jnp.concatenate(parts(v), axis=1)
    return jnp.concatenate([both, both], axis=0)


def left_lanes(shape):
    return lax.broadcasted_iota(jnp.int32, shape, 1) < shape[1] // 2


def gram_kernel(x_ref, gram_ref, terms_ref):
    step = pl.program_id(0)

    @pl.when(step == 0)
    def _():
        terms_ref[...] = jnp.zeros_like(terms_ref)

    terms_ref[...] += gram_terms(x_ref[...])

    @pl.when(step == pl.num_programs(0) - 1)
    def _():
        gram_ref[...] = gram_of_terms(terms_ref[...])


def local_gram(x, block):
    rows, width = x.shape
    return pl.pallas_call(
        gram_kernel,
        grid=(rows // block,),
        in_specs=[pl.BlockSpec((block, width), lambda i: (i, 0))],
        out_specs=pl.BlockSpec((width, width), lambda i: (0, 0)),
        out_shape=jax.ShapeDtypeStruct((width, width), F32),
        scratch_shapes=[pltpu.VMEM((width, 2 * width), F32)],
        cost_estimate=HINT,
        compiler_params=params(),
    )(x)


def rotation_kernel(which, flags_ref, offsets_ref, one_ref, two_ref, a_ref, b_ref):
    gram = one_ref[...] + two_ref[...]
    width = gram.shape[0]
    half = width // 2
    row = lax.broadcasted_iota(jnp.int32, (width, width), 0)
    lane = lax.broadcasted_iota(jnp.int32, (width, width), 1)
    eye = row == lane
    is_first = lax.broadcasted_iota(jnp.int32, (1, width), 1) < half
    vectors = jnp.where(eye, 1.0, 0.0).astype(F32)
    dot = functools.partial(
        jnp.dot, precision=lax.Precision.HIGHEST, preferred_element_type=F32
    )
    for turn in range(ROUNDS):
        offset = offsets_ref[which, turn]
        above = lane + offset
        above = half + jnp.where(above >= half, above - half, above)
        below = lane - half - offset
        below = jnp.where(below < 0, below + half, below)
        pair = row == jnp.where(lane < half, above, below)
        own = jnp.sum(jnp.where(eye, gram, 0.0), axis=0, keepdims=True)
        own_col = jnp.sum(jnp.where(eye, gram, 0.0), axis=1, keepdims=True)
        other = jnp.sum(jnp.where(pair, own_col, 0.0), axis=0, keepdims=True)
        cross = jnp.sum(jnp.where(pair, gram, 0.0), axis=0, keepdims=True)
        spread = jnp.where(is_first, other - own, own - other)
        sign = jnp.where(spread >= 0.0, 1.0, -1.0)
        tangent = (
            sign
            * 2.0
            * cross
            / (jnp.abs(spread) + jnp.sqrt(spread * spread + 4.0 * cross * cross))
        )
        cosine = 1.0 / jnp.sqrt(1.0 + tangent * tangent)
        sine = tangent * cosine
        signed = jnp.where(is_first, -sine, sine)
        on_diagonal = jnp.where(eye, cosine, 0.0)
        off_diagonal = jnp.where(pair, signed, 0.0)
        turned = on_diagonal + off_diagonal
        vectors = dot(vectors, turned)
        if turn < ROUNDS - 1:
            gram = dot(on_diagonal - off_diagonal, dot(gram, turned))
    if which == 0:
        vectors = jnp.where(flags_ref[0] == 1, swapped(vectors, 1), vectors)
        other_vectors = swapped(vectors, 1)
    else:
        other_vectors = swapped(vectors, 0)
    a_ref[...] = weights_of(vectors)
    b_ref[...] = weights_of(other_vectors)


def rotations(which, flags, offsets, one, two):
    width = one.shape[0]
    smem = pl.BlockSpec(memory_space=pltpu.SMEM)
    vmem = pl.BlockSpec(memory_space=pltpu.VMEM)
    return pl.pallas_call(
        functools.partial(rotation_kernel, which),
        in_specs=[smem, smem, vmem, vmem],
        out_specs=[vmem, vmem],
        out_shape=[jax.ShapeDtypeStruct((2 * width, 2 * width), BF16)] * 2,
        cost_estimate=HINT,
        compiler_params=params(8),
    )(flags, offsets, one, two)


def run_spec(low, count, block, width):
    return pl.BlockSpec(
        (block, width), lambda i, f: (jnp.clip(i - low, 0, count - 1), 0)
    )


def first_product_kernel(runs, flags_ref, x_ref, a_ref, b_ref, *out_refs):
    ya = times(x_ref[0], a_ref[...])
    yb = times(x_ref[1], b_ref[...])
    left = left_lanes(ya.shape)
    up = jnp.where(left, ya, yb)
    down = jnp.where(left, yb, ya)
    step = pl.program_id(0)
    for which, (low, count) in enumerate(runs):

        @pl.when((step >= low) & (step < low + count))
        def _():
            out_refs[2 * which][...] = up
            out_refs[2 * which + 1][...] = down

    @pl.when(step >= runs[-1][0])
    def _():
        out_refs[-1][...] = jnp.where(flags_ref[2] == 1, down, up)


def first_product(flags, x, a, b, block, runs):
    width = x.shape[2]
    steps = sum(count for _, count in runs)
    whole = pl.BlockSpec(a.shape, lambda i, f: (0, 0))
    out_specs, out_shape = [], []
    for low, count in [run for run in runs for _ in range(2)] + runs[-1:]:
        out_specs.append(run_spec(low, count, block, width))
        out_shape.append(jax.ShapeDtypeStruct((count * block, width), F32))
    return pl.pallas_call(
        functools.partial(first_product_kernel, runs),
        grid_spec=pltpu.PrefetchScalarGridSpec(
            num_scalar_prefetch=1,
            grid=(steps,),
            in_specs=[
                pl.BlockSpec((2, block, width), lambda i, f: (0, i, 0)),
                whole,
                whole,
            ],
            out_specs=out_specs,
        ),
        out_shape=out_shape,
        cost_estimate=HINT,
        compiler_params=params(52),
    )(flags, x, a, b)


def packed_gram_kernel(halves, flags_ref, *refs):
    *in_refs, gram_ref, a_ref, b_ref = refs
    step = pl.program_id(0)

    @pl.when(step == 0)
    def _():
        a_ref[...] = jnp.zeros_like(a_ref)
        b_ref[...] = jnp.zeros_like(b_ref)

    def add(first, second):
        left = left_lanes(first.shape)
        a_ref[...] += gram_terms(jnp.where(left, first, second))
        b_ref[...] += gram_terms(jnp.where(left, second, first))

    halves(step, flags_ref, add, *in_refs)

    @pl.when(step == pl.num_programs(0) - 1)
    def _():
        other = gram_of_terms(b_ref[...])
        gram_ref[...] = gram_of_terms(a_ref[...]) + swapped(swapped(other, 0), 1)


def neighbour_halves(step, flags_ref, add, got_ref, u_ref, w_ref):
    own = jnp.where(flags_ref[2] == 1, u_ref[...], w_ref[...])
    at_end = flags_ref[0] + flags_ref[1]
    own = jnp.where(at_end == 1, swapped(own, 1), own)
    got = got_ref[...]
    own_first = flags_ref[3] == 1
    add(jnp.where(own_first, own, got), jnp.where(own_first, got, own))


def arrived_halves(step, flags_ref, add, up_ref, down_ref, u_ref, w_ref):
    bottom = flags_ref[0] == 1
    top = flags_ref[1] == 1

    @pl.when(jnp.logical_not(jnp.logical_or(bottom, top)))
    def _():
        add(up_ref[...], down_ref[...])

    @pl.when(bottom)
    def _():
        add(swapped(w_ref[...], 1), down_ref[...])

    @pl.when(top)
    def _():
        add(up_ref[...], swapped(u_ref[...], 1))


def skipped_halves(step, flags_ref, add, up_ref, down_ref, u_ref, w_ref, got_ref):
    bottom = flags_ref[0] == 1
    top = flags_ref[1] == 1

    @pl.when(jnp.logical_not(jnp.logical_or(bottom, top)))
    def _():
        add(up_ref[...], down_ref[...])

    @pl.when(bottom)
    def _():
        add(swapped(w_ref[...], 1), got_ref[...])

    @pl.when(top)
    def _():
        add(got_ref[...], swapped(u_ref[...], 1))


def gram_call(halves, flags, operands, specs, steps):
    width = operands[0].shape[1]
    return pl.pallas_call(
        functools.partial(packed_gram_kernel, halves),
        grid_spec=pltpu.PrefetchScalarGridSpec(
            num_scalar_prefetch=1,
            grid=(steps,),
            in_specs=specs,
            out_specs=pl.BlockSpec((width, width), lambda i, f: (0, 0)),
            scratch_shapes=[pltpu.VMEM((width, 2 * width), F32)] * 2,
        ),
        out_shape=jax.ShapeDtypeStruct((width, width), F32),
        cost_estimate=HINT,
        compiler_params=params(),
    )(flags, *operands)


def neighbour_gram(flags, got, u, w, block):
    rows, width = got.shape
    steps = rows // block
    every = run_spec(0, steps, block, width)
    return gram_call(neighbour_halves, flags, [got, u, w], [every] * 3, steps)


def kept_spec(block, width):
    return pl.BlockSpec((block, width), lambda i, f: (i * (f[0] + f[1]), 0))


def arrived_gram(flags, up, down, u, w, block):
    rows, width = up.shape
    steps = rows // block
    every = run_spec(0, steps, block, width)
    kept = kept_spec(block, width)
    return gram_call(
        arrived_halves, flags, [up, down, u, w], [every, every, kept, kept], steps
    )


def second_product_kernel(halves, count, flags_ref, a_ref, b_ref, *refs):
    out_ref = refs[-1]

    def finish(first, second):
        left = left_lanes(first.shape)
        out_ref[0] = times(jnp.where(left, first, second), a_ref[...])
        out_ref[1] = times(jnp.where(left, second, first), b_ref[...])

    halves(pl.program_id(0), flags_ref, finish, *refs[:count])


def second_product(flags, a, b, operands, got, got_start, out, start, total, block):
    rows, width = operands[0].shape
    first = start // block
    got_first = got_start // block
    every = run_spec(0, rows // block, block, width)
    kept = kept_spec(block, width)
    whole = pl.BlockSpec(a.shape, lambda i, f: (0, 0))
    in_specs = [whole, whole, every, every, kept, kept]
    operands = list(operands)
    halves = arrived_halves
    if got is not None:
        halves = skipped_halves
        operands.append(got)
        in_specs.append(
            pl.BlockSpec(
                (block, width), lambda i, f: ((i + got_first) * (f[0] + f[1]), 0)
            )
        )
    count = len(operands)
    aliases = {}
    if out is not None:
        aliases = {3 + count: 0}
        operands.append(out)
        in_specs.append(pl.BlockSpec(memory_space=pl.ANY))
    return pl.pallas_call(
        functools.partial(second_product_kernel, halves, count),
        grid_spec=pltpu.PrefetchScalarGridSpec(
            num_scalar_prefetch=1,
            grid=(rows // block,),
            in_specs=in_specs,
            out_specs=pl.BlockSpec((2, block, width), lambda i, f: (0, i + first, 0)),
        ),
        out_shape=jax.ShapeDtypeStruct((2, total, width), F32),
        input_output_aliases=aliases,
        cost_estimate=HINT,
        compiler_params=params(52),
    )(flags, a, b, *operands)


def row_partner(x, bit):
    size = lax.axis_size("rows")
    return lax.ppermute(x, "rows", [(i, i ^ bit) for i in range(size)])


def everywhere(x, target):
    rows, places = lax.axis_size("rows"), lax.axis_size("loop")
    pairs = []
    for row in range(rows):
        for place in range(places):
            where = target(row, place)
            pairs.append((row * places + place, where[0] * places + where[1]))
    return lax.ppermute(x, ("rows", "loop"), pairs)


def home(x, last):
    def onward(row, place):
        if place == 1:
            return row ^ 2, 0
        if place == last - 1:
            return row ^ 2, last
        return row, place - 2 if place % 2 else place + 2

    x = everywhere(x, lambda row, place: (row ^ 2, place ^ 1))
    return everywhere(x, onward)


def far_partner(x, count):
    ring = min(4, count // 2)

    def across(place):
        pair, odd = divmod(place, 2)
        group, at = divmod(pair, ring)
        at = (at - 1) % ring if odd else (at + 1) % ring
        return 2 * (group * ring + at) + 1 - odd

    x = everywhere(x, lambda row, place: (row, across(place)))
    return everywhere(x, lambda row, place: (row ^ 2, across(place)))


def held_kernel(*refs):
    pass


def held(arrays, earlier):
    anywhere = pl.BlockSpec(memory_space=pl.ANY)
    return pl.pallas_call(
        held_kernel,
        in_specs=[anywhere] * (len(arrays) + 1),
        out_specs=[anywhere] * len(arrays),
        out_shape=[jax.ShapeDtypeStruct(x.shape, x.dtype) for x in arrays],
        input_output_aliases={k: k for k in range(len(arrays))},
        cost_estimate=HINT,
        compiler_params=params(),
    )(*arrays, earlier)


def body(x, offsets):
    rows, width = x.shape
    half_rows = rows // 2
    block = half_rows // 6
    late = 4 * block
    place = lax.axis_index("loop")
    count = lax.axis_size("loop")
    last = count - 1
    odd = place % 2
    flags = jnp.stack(
        [
            (place == 0).astype(jnp.int32),
            (place == last).astype(jnp.int32),
            odd.astype(jnp.int32),
            ((place == 0) | ((odd == 1) & (place != last))).astype(jnp.int32),
        ]
    )
    halves = x.reshape(2, half_rows, width)

    ups = [(i, i + 1) for i in range(last)]
    downs = [(i, i - 1) for i in range(1, count)]
    skips = (
        [(i, i + 2) for i in range(0, last - 1, 2)]
        + [(i, i - 2) for i in range(3, count, 2)]
    )
    by_down, by_up = (25, 6) if count == 32 else (1, last - 1)

    gram = local_gram(x, rows // 3)
    gram = gram + row_partner(gram, 1)
    a, b = rotations(0, flags, offsets, gram, row_partner(gram, 2))

    u0, w0, u1, w1, sent = first_product(
        flags, halves, a, b, block, [(0, 4), (4, 2)]
    )
    up0 = lax.ppermute(u0, "loop", ups)
    down0 = lax.ppermute(w0, "loop", downs)
    got = lax.ppermute(sent, "loop", skips)
    ends = lax.ppermute(sent, "loop", [(1, by_down), (last - 1, by_up)])
    (ends,) = held([ends], got)
    ends = lax.ppermute(ends, "loop", [(by_down, 0), (by_up, last)])
    u1, w1 = held([u1, w1], got)
    up1 = lax.ppermute(u1, "loop", ups[:-1])
    down1 = lax.ppermute(w1, "loop", downs[1:])
    got = jnp.where((place == 0) | (place == last), ends, got)

    gram = neighbour_gram(flags, got, u1, w1, block)
    (gram,) = held([gram], up0)
    (gram,) = held([gram], down0)
    gram = home(gram, last)
    gram = gram + arrived_gram(flags, up0, down0, u0, w0, block)
    gram = gram + row_partner(gram, 1)
    a, b = rotations(1, flags, offsets, gram, far_partner(gram, count))

    out = second_product(
        flags, a, b, (up0, down0, u0, w0), None, 0, None, 0, half_rows, block
    )
    out = second_product(
        flags, a, b, (up1, down1, u1, w1), got, 0, out, late, half_rows, block
    )
    return out.reshape(rows, width)


def solution(mesh):
    placed = (P("rows", "loop"), P())
    return jax.shard_map(
        body,
        mesh=mesh,
        in_specs=placed,
        out_specs=P("rows", "loop"),
        check_vma=False,
    )
```
